32 devices in a mesh: dp: 4 (over y, x), tensor: 8 (over z, core).
Axes of the slice: x: 2, y: 2, z: 4, core: 2. Of those that a mesh axis runs over, the one named last changes fastest.
Arguments:
- inputs: bfloat16 [4096, 8192], P(('dp', 'tensor')), may hold values from -6 to 6
- queries: bfloat16 [4096, 6144], P('dp', 'tensor'), may hold values from -6 to 6
- keys_values: bfloat16 [4096, 1024], P('dp', 'tensor'), may hold values from -6 to 6
- out_grad: bfloat16 [4096, 6144], P('dp', 'tensor'), may hold values from -6 to 6
- weight_mask: int32 [8192, 1024], P('dp', 'tensor'), may hold values 0 or 1
- clip_mask: int32 [4096, 8], P('dp', 'tensor'), may hold values 0 or 1
Outputs:
- query_grad: bfloat16 [4096, 6144], P('dp', 'tensor')
- weight_grad: float32 [8192, 1024], P('dp', 'tensor')
The draws below stay inside these ranges and needn't reach their ends.
All inputs are finite; a program needn't handle non-finite values. No bound on the sum of `weight_mask` or of `clip_mask` on one device may be relied on, other than what follows from the above.
Results may differ from the reference program's by a relative error of at most 0.0056.
Values may be sent and summed in bfloat16 or wider, within the bound.
No kernel may reach another device: no remote copies, remote signals or barrier semaphores. Data moves between devices by JAX's collectives and lax.ppermute only.
A program may use at most 192 MiB of HBM per device.

```python
import jax
import jax.numpy as jnp
from jax import lax

D = 8192
HD = 128
SEQ = 1024
TOKENS = 4096
HQ = 48
KVH = 4
N_DP = 4


def draw_queries(key, part):
    key = jax.random.fold_in(key, 3)
    values = jnp.clip(jax.random.normal(key, (TOKENS, HQ * HD), jnp.float32), -6.0, 6.0)
    return values.astype(jnp.bfloat16)


def draw_keys_values(key, part):
    key = jax.random.fold_in(key, 5)
    values = jnp.clip(jax.random.normal(key, (TOKENS, 2 * KVH * HD), jnp.float32), -6.0, 6.0)
    return values.astype(jnp.bfloat16)


def plant(entries, stream_key, least, top_value):
    shape = entries.shape
    place = [jax.random.randint(jax.random.fold_in(stream_key, axis), (), 0, shape[axis]) for axis in range(len(shape))]
    entries = entries.at[tuple(place)].set(least)
    longest = shape.index(max(shape))
    place[longest] = (place[longest] + 1) % shape[longest]
    return entries.at[tuple(place)].set(top_value)


def block_scale(rng, shape, shards, least, high):
    def one(dim, parts):
        heights = jax.random.uniform(jax.random.fold_in(jax.random.fold_in(rng, 6), dim), (parts,), jnp.float32, least / len(shards), high / len(shards))
        return jnp.repeat(jnp.exp(heights), shape[dim] // parts).reshape((-1,) + (1,) * (len(shape) - dim - 1))

    gain = one(*shards[0])
    for cut in shards[1:]:
        gain = gain * one(*cut)
    return gain


def bell_draw(own_key, dims, deviation, bound, shards=(), dtype=jnp.bfloat16):
    gain = block_scale(own_key, dims, shards, -0.22, 0.18) if shards else 1.0
    entries = jax.random.normal(own_key, dims, jnp.float32) * deviation * gain
    return jnp.minimum(jnp.maximum(entries, -bound), bound).astype(dtype)


def setup_inputs(seed: int = 0) -> dict:
    key_list = jax.random.split(jax.random.key(seed), 7)
    inputs = bell_draw(key_list[0], (TOKENS, D), 1.0, 6.0, ((0, 32),))
    queries = draw_queries(jax.random.fold_in(key_list[6], 71), 0)
    keys_values = draw_keys_values(jax.random.fold_in(key_list[6], 71), 0)
    out_grad = bell_draw(key_list[3], (TOKENS, HQ * HD), 1.0, 6.0, ((0, 4), (1, 8)))
    weight_mask = plant((jax.random.randint(key_list[4], (D, 2 * KVH * HD), 0, 4) < 3).astype(jnp.int32), jax.random.fold_in(key_list[4], 1), 0, 1)
    clip_mask = plant((jax.random.randint(key_list[5], (TOKENS, 2 * KVH), 0, 4) < 3).astype(jnp.int32), jax.random.fold_in(key_list[5], 1), 0, 1)
    return dict(inputs=inputs, queries=queries, keys_values=keys_values, out_grad=out_grad, weight_mask=weight_mask, clip_mask=clip_mask)


def head_backward(query, keys, values, upstream):
    length = query.shape[0]
    height = min(512, length)
    factor = query.shape[1] ** -0.5
    query_pieces = []
    key_grad = jnp.zeros(keys.shape, jnp.float32)
    value_grad = jnp.zeros(values.shape, jnp.float32)
    for block in range(length // height):
        first = block * height
        finish = first + height
        query_block = query[first:finish]
        upstream_block = upstream[first:finish]
        key_block = keys[:finish]
        value_block = values[:finish]
        scores = jnp.dot(query_block, key_block.T, preferred_element_type=jnp.float32) * factor
        row_place = first + lax.broadcasted_iota(jnp.int32, scores.shape, 0)
        col_place = lax.broadcasted_iota(jnp.int32, scores.shape, 1)
        scores = jnp.where(col_place <= row_place, scores, -jnp.inf)
        biggest = jnp.max(scores, axis=1, keepdims=True)
        weights = jnp.exp(scores - biggest)
        weights = weights / jnp.sum(weights, axis=1, keepdims=True)
        weights_half = weights.astype(jnp.bfloat16)
        value_grad = value_grad.at[:finish].add(jnp.dot(weights_half.T, upstream_block, preferred_element_type=jnp.float32))
        product = jnp.dot(upstream_block, value_block.T, preferred_element_type=jnp.float32)
        center = jnp.sum(weights * product, axis=1, keepdims=True)
        score_grad = (weights * (product - center) * factor).astype(jnp.bfloat16)
        query_pieces.append(jnp.dot(score_grad, key_block, preferred_element_type=jnp.float32))
        key_grad = key_grad.at[:finish].add(jnp.dot(score_grad.T, query_block, preferred_element_type=jnp.float32))
    return jnp.concatenate(query_pieces, 0).astype(jnp.bfloat16), key_grad, value_grad


def one_head(items):
    return head_backward(items[0], items[1], items[2], items[3])


def reference(inputs, queries, keys_values, out_grad, weight_mask, clip_mask):
    group = HQ // KVH
    weight_total = jnp.zeros((D, 2 * KVH * HD), jnp.float32)
    query_parts = []
    for sequence in range(N_DP):
        first = sequence * SEQ
        finish = first + SEQ
        query_seq = queries[first:finish].reshape(SEQ, HQ, HD).transpose(1, 0, 2)
        upstream_seq = out_grad[first:finish].reshape(SEQ, HQ, HD).transpose(1, 0, 2)
        paired = keys_values[first:finish].reshape(SEQ, KVH, 2, HD)
        key_heads = jnp.repeat(paired[:, :, 0].transpose(1, 0, 2), group, axis=0)
        value_heads = jnp.repeat(paired[:, :, 1].transpose(1, 0, 2), group, axis=0)
        query_grad, key_grad, value_grad = lax.map(one_head, (query_seq, key_heads, value_heads, upstream_seq))
        key_sum = key_grad.reshape(KVH, group, SEQ, HD).sum(axis=1)
        value_sum = value_grad.reshape(KVH, group, SEQ, HD).sum(axis=1)
        stacked = jnp.stack([key_sum, value_sum], axis=1).transpose(2, 0, 1, 3).reshape(SEQ, 2 * KVH * HD)
        masks = jnp.repeat(clip_mask[first:finish].astype(jnp.float32), HD, axis=1)
        kv_grad = (stacked * masks).astype(jnp.bfloat16)
        weight_total = weight_total + jnp.dot(inputs[first:finish].T, kv_grad, preferred_element_type=jnp.float32)
        query_parts.append(query_grad.transpose(1, 0, 2).reshape(SEQ, HQ * HD))
    weight_grad = jnp.where(weight_mask == 1, weight_total, jnp.zeros_like(weight_total))
    return jnp.concatenate(query_parts, 0), weight_grad
```

```python
import functools
import math

import jax
import jax.numpy as jnp
from jax import lax
from jax.experimental import pallas as pl
from jax.experimental.pallas import tpu as pltpu
from jax.sharding import PartitionSpec as P

F32 = jnp.float32
BF16 = jnp.bfloat16
VMEM_LIMIT = 56 * 2**20


def swap(value, axis, mask):
    pairs = [(source, source ^ mask) for source in range(lax.axis_size(axis))]
    return lax.ppermute(value, axis, pairs)


def dot(left, right, left_dim, right_dim):
    dims = (((left_dim,), (right_dim,)), ((), ()))
    return lax.dot_general(left, right, dims, preferred_element_type=F32)


def attention_kernel(height, own_ref, other_ref, q_ref, up_ref, dq_ref, mine_ref, theirs_ref, k_ref, v_ref, dk_ref, dv_ref):
    length, depth = q_ref.shape
    factor = depth**-0.5
    power = factor * math.log2(math.e)
    head = pl.program_id(0)
    is_even = lax.axis_index("tensor") % 2 == 0

    @pl.when(head == 0)
    def _():
        k_ref[...] = jnp.where(is_even, own_ref[...], other_ref[...])
        v_ref[...] = jnp.where(is_even, other_ref[...], own_ref[...])
        dk_ref[...] = jnp.zeros_like(dk_ref)
        dv_ref[...] = jnp.zeros_like(dv_ref)

    for block in reversed(range(length // height)):
        first = block * height
        finish = first + height
        query = q_ref[first:finish]
        upstream = up_ref[first:finish]
        keys = k_ref[:finish]
        values = v_ref[:finish]
        scores = dot(keys, query, 1, 1)
        key_place = lax.broadcasted_iota(jnp.int32, (height, height), 0)
        query_place = lax.broadcasted_iota(jnp.int32, (height, height), 1)
        corner = jnp.where(key_place <= query_place, scores[first:], -jnp.inf)
        scores = corner if block == 0 else jnp.concatenate([scores[:first], corner], 0)
        biggest = jnp.max(scores, axis=0, keepdims=True)
        weights = jnp.exp2((scores - biggest) * power)
        weights = weights * (1.0 / jnp.sum(weights, axis=0, keepdims=True))
        product = dot(values, upstream, 1, 1)
        center = jnp.sum(weights * product, axis=0, keepdims=True)
        score_grad = (weights * (product - center) * factor).astype(BF16)
        dv_ref[:finish] += dot(weights.astype(BF16), upstream, 1, 0)
        dk_ref[:finish] += dot(score_grad, query, 1, 0)
        dq_ref[first:finish] = dot(score_grad, keys, 0, 0).astype(BF16)

    @pl.when(head == pl.num_programs(0) - 1)
    def _():
        mine_ref[...] = jnp.where(is_even, dk_ref[...], dv_ref[...])
        theirs_ref[...] = jnp.where(is_even, dv_ref[...], dk_ref[...])


def attention(own, other, queries, out_grad):
    length, width = queries.shape
    depth = own.shape[1]
    height = min(512, length)
    column = pl.BlockSpec((length, depth), lambda h: (0, h))
    whole = pl.BlockSpec((length, depth), lambda h: (0, 0))
    sums = jax.ShapeDtypeStruct((length, depth), F32)
    return pl.pallas_call(
        functools.partial(attention_kernel, height),
        grid=(width // depth,),
        in_specs=[whole, whole, column, column],
        out_specs=[column, whole, whole],
        out_shape=[jax.ShapeDtypeStruct((length, width), BF16), sums, sums],
        scratch_shapes=[
            pltpu.VMEM((length, depth), BF16),
            pltpu.VMEM((length, depth), BF16),
            pltpu.VMEM((length, depth), F32),
            pltpu.VMEM((length, depth), F32),
        ],
        compiler_params=pltpu.CompilerParams(
            vmem_limit_bytes=VMEM_LIMIT, dimension_semantics=("arbitrary",)
        ),
        name="attention",
    )(own, other, queries, out_grad)


def kv_kernel(rows, mine_ref, arrived_ref, mask_ref, out_ref):
    place = lax.axis_index("tensor")
    chip, core = place // 2, place % 2
    for step in range(out_ref.shape[0]):
        for half in range(2):
            start = ((chip ^ step) * 2 + (core ^ half)) * rows
            span = pl.ds(pl.multiple_of(start, rows), rows)
            total = (mine_ref[span, :] + arrived_ref[span, :]).T
            keep = mask_ref[:, span].astype(F32)
            out_ref[step, :, half * rows : (half + 1) * rows] = (total * keep).astype(BF16)


def kv_blocks(mine, arrived, mask, rows):
    length, depth = mine.shape
    return pl.pallas_call(
        functools.partial(kv_kernel, rows),
        out_shape=jax.ShapeDtypeStruct((length // (2 * rows), depth, 2 * rows), BF16),
        compiler_params=pltpu.CompilerParams(vmem_limit_bytes=VMEM_LIMIT),
        name="kv_blocks",
    )(mine, arrived, mask)


def project_kernel(parts, *refs):
    out_ref = refs[-1]
    total = None
    for part in range(parts):
        grads = refs[2 * parts + part]
        rows = refs[0].shape[0]
        for half in range(2):
            term = dot(grads[:, half * rows : (half + 1) * rows], refs[2 * part + half][...], 1, 0)
            total = term if total is None else total + term
    out_ref[...] = total.astype(out_ref.dtype)


def project(pairs, grads, first, wide, dtype, tile):
    rows = pairs[0][0].shape[0]
    height, tokens = grads[0].shape
    skip = first // tile
    in_specs = [pl.BlockSpec((rows, tile), lambda j: (0, j + skip)) for _ in range(2 * len(pairs))]
    in_specs += [pl.BlockSpec((height, tokens), lambda j: (0, 0)) for _ in grads]
    return pl.pallas_call(
        functools.partial(project_kernel, len(pairs)),
        grid=(wide // tile,),
        in_specs=in_specs,
        out_specs=pl.BlockSpec((height, tile), lambda j: (0, j)),
        out_shape=jax.ShapeDtypeStruct((height, wide), dtype),
        compiler_params=pltpu.CompilerParams(
            vmem_limit_bytes=VMEM_LIMIT, dimension_semantics=("arbitrary",)
        ),
        name="project",
    )(*[x for pair in pairs for x in pair], *grads)


def finish_kernel(parts, *refs):
    total = refs[0][...]
    for part in range(1, parts):
        total = total + refs[part][...].astype(F32)
    refs[-1][...] = jnp.where(refs[parts][...] == 1, total.T, 0.0)


def finish(terms, weight_mask, tile):
    depth = terms[0].shape[0]
    height = weight_mask.shape[0]
    across = pl.BlockSpec((depth, tile), lambda j: (0, j))
    down = pl.BlockSpec((tile, depth), lambda j: (j, 0))
    return pl.pallas_call(
        functools.partial(finish_kernel, len(terms)),
        grid=(height // tile,),
        in_specs=[across] * len(terms) + [down],
        out_specs=down,
        out_shape=jax.ShapeDtypeStruct((height, depth), F32),
        compiler_params=pltpu.CompilerParams(
            vmem_limit_bytes=VMEM_LIMIT, dimension_semantics=("arbitrary",)
        ),
        name="finish",
    )(*terms, weight_mask)


def per_device(inputs, queries, keys_values, out_grad, weight_mask, clip_mask):
    depth = keys_values.shape[1]
    rows = inputs.shape[0]
    groups = lax.axis_size("dp")
    chips = lax.axis_size("tensor") // 2
    block = weight_mask.shape[0]
    row_place = lax.axis_index("dp")

    other = swap(keys_values, "tensor", 1)
    mine_rows = []
    for step in range(groups):
        start = (row_place ^ step) * block
        part = lax.dynamic_slice(inputs, (0, start), (rows, block))
        mine_rows.append(part if step == 0 else swap(part, "dp", step))
    pairs = [(part, swap(part, "tensor", 1)) for part in mine_rows]

    query_grad, mine, theirs = attention(keys_values, other, queries, out_grad)
    arrived = swap(theirs, "tensor", 1)
    blocks = kv_blocks(mine, arrived, clip_mask.reshape(1, -1), rows)

    def column(step):
        return blocks[step] if step == 0 else swap(blocks[step], "tensor", 2 * step)

    order = sorted(range(chips), key=lambda s: [(s >> b) & 1 for b in range(8)])
    stacked = jnp.concatenate([column(step) for step in order], 0)
    grads = [stacked if step == 0 else swap(stacked, "dp", step) for step in range(groups)]

    cuts = 2 if block % 1024 == 0 else 1
    wide = block // cuts
    tile = min(512, wide)
    half = chips // 2 * depth
    pieces = []
    for cut in range(cuts):
        away = project(pairs, [g[half:] for g in grads], cut * wide, wide, BF16, tile)
        pieces.append(swap(away, "tensor", 2))
    kept = project(pairs, [g[:half] for g in grads], 0, block, F32, tile)
    finals = []
    for cut in range(cuts):
        own = kept[:, cut * wide : (cut + 1) * wide]
        terms = [own, pieces[cut]]
        size, bit = half, 2
        while size > depth:
            size, bit = size // 2, bit * 2
            away = sum(t[size:].astype(F32) for t in terms).astype(BF16)
            terms = [t[:size] for t in terms] + [swap(away, "tensor", bit)]
        finals.append(terms)
    merged = [jnp.concatenate([f[k] for f in finals], 1) for k in range(len(finals[0]))]
    weight_grad = finish(merged, weight_mask, min(512, block))
    return (query_grad, weight_grad)


def solution(mesh):
    spec = P("dp", "tensor")
    in_specs = (P(("dp", "tensor"), None), spec, spec, spec, spec, spec)
    return jax.shard_map(
        per_device, mesh=mesh, in_specs=in_specs, out_specs=(spec, spec), check_vma=False
    )
```

```python
import functools
import math

import jax
import jax.numpy as jnp
from jax import lax
from jax.experimental import pallas as pl
from jax.experimental.pallas import tpu as pltpu
from jax.sharding import PartitionSpec as P

F32 = jnp.float32
BF16 = jnp.bfloat16
VMEM_LIMIT = 56 * 2**20
IN_ORDER = pltpu.CompilerParams(
    vmem_limit_bytes=VMEM_LIMIT, dimension_semantics=("arbitrary",)
)


def cost(flops, moved, exponents=0):
    return pl.CostEstimate(flops=flops, bytes_accessed=moved, transcendentals=exponents)


def swap(value, axis, mask):
    pairs = [(source, source ^ mask) for source in range(lax.axis_size(axis))]
    return lax.ppermute(value, axis, pairs)


def dot(left, right, left_dim, right_dim):
    dims = (((left_dim,), (right_dim,)), ((), ()))
    return lax.dot_general(left, right, dims, preferred_element_type=F32)


def attention_kernel(height, own_ref, other_ref, q_ref, up_ref, dq_ref, mine_ref, theirs_ref, k_ref, v_ref, dk_ref, dv_ref):
    length, depth = q_ref.shape
    factor = depth**-0.5
    power = factor * math.log2(math.e)
    head = pl.program_id(0)
    is_even = lax.axis_index("tensor") % 2 == 0

    @pl.when(head == 0)
    def _():
        k_ref[...] = jnp.where(is_even, own_ref[...], other_ref[...])
        v_ref[...] = jnp.where(is_even, other_ref[...], own_ref[...])
        dk_ref[...] = jnp.zeros_like(dk_ref)
        dv_ref[...] = jnp.zeros_like(dv_ref)

    for block in reversed(range(length // height)):
        first = block * height
        finish = first + height
        query = q_ref[first:finish]
        upstream = up_ref[first:finish]
        keys = k_ref[:finish]
        values = v_ref[:finish]
        scores = dot(keys, query, 1, 1)
        key_place = lax.broadcasted_iota(jnp.int32, (height, height), 0)
        query_place = lax.broadcasted_iota(jnp.int32, (height, height), 1)
        corner = jnp.where(key_place <= query_place, scores[first:], -jnp.inf)
        scores = corner if block == 0 else jnp.concatenate([scores[:first], corner], 0)
        biggest = jnp.max(scores, axis=0, keepdims=True)
        weights = jnp.exp2((scores - biggest) * power)
        weights = weights * (1.0 / jnp.sum(weights, axis=0, keepdims=True))
        product = dot(values, upstream, 1, 1)
        center = jnp.sum(weights * product, axis=0, keepdims=True)
        score_grad = (weights * (product - center) * factor).astype(BF16)
        dv_ref[:finish] += dot(weights.astype(BF16), upstream, 1, 0)
        dk_ref[:finish] += dot(score_grad, query, 1, 0)
        dq_ref[first:finish] = dot(score_grad, keys, 0, 0).astype(BF16)

    @pl.when(head == pl.num_programs(0) - 1)
    def _():
        mine_ref[...] = jnp.where(is_even, dk_ref[...], dv_ref[...])
        theirs_ref[...] = jnp.where(is_even, dv_ref[...], dk_ref[...])


def attention(own, other, queries, out_grad):
    length, width = queries.shape
    depth = own.shape[1]
    height = min(512, length)
    column = pl.BlockSpec((length, depth), lambda h: (0, h))
    whole = pl.BlockSpec((length, depth), lambda h: (0, 0))
    sums = jax.ShapeDtypeStruct((length, depth), F32)
    return pl.pallas_call(
        functools.partial(attention_kernel, height),
        grid=(width // depth,),
        in_specs=[whole, whole, column, column],
        out_specs=[column, whole, whole],
        out_shape=[jax.ShapeDtypeStruct((length, width), BF16), sums, sums],
        scratch_shapes=[
            pltpu.VMEM((length, depth), BF16),
            pltpu.VMEM((length, depth), BF16),
            pltpu.VMEM((length, depth), F32),
            pltpu.VMEM((length, depth), F32),
        ],
        compiler_params=IN_ORDER,
        cost_estimate=cost(
            20 * length * length * width,
            6 * queries.nbytes,
            length * length * width // depth,
        ),
        name="attention",
    )(own, other, queries, out_grad)


def kv_kernel(rows, mine_ref, arrived_ref, mask_ref, *out_refs):
    place = lax.axis_index("tensor")
    chip, core = place // 2, place % 2
    for step, out_ref in enumerate(out_refs):
        for half in range(2):
            start = ((chip ^ step) * 2 + (core ^ half)) * rows
            span = pl.ds(pl.multiple_of(start, rows), rows)
            total = mine_ref[span, :] + arrived_ref[span, :].astype(F32)
            keep = mask_ref[span, :].astype(F32)
            out_ref[half * rows : (half + 1) * rows, :] = (total * keep).astype(BF16)


def kv_blocks(mine, arrived, mask, rows):
    length, depth = mine.shape
    count = length // (2 * rows)
    return pl.pallas_call(
        functools.partial(kv_kernel, rows),
        out_shape=[jax.ShapeDtypeStruct((2 * rows, depth), BF16)] * count,
        compiler_params=pltpu.CompilerParams(vmem_limit_bytes=VMEM_LIMIT),
        cost_estimate=cost(0, 2 * mine.nbytes),
        name="kv_blocks",
    )(mine, arrived, mask)


def turn_kernel(first_ref, second_ref, out_ref):
    rows = first_ref.shape[0]
    out_ref[:, :rows] = first_ref[...].T
    out_ref[:, rows:] = second_ref[...].T


def turn(first, second):
    rows, wide = first.shape
    tile = min(512, wide)
    return pl.pallas_call(
        turn_kernel,
        grid=(wide // tile,),
        in_specs=[pl.BlockSpec((rows, tile), lambda j: (0, j))] * 2,
        out_specs=pl.BlockSpec((tile, 2 * rows), lambda j: (j, 0)),
        out_shape=jax.ShapeDtypeStruct((wide, 2 * rows), first.dtype),
        compiler_params=IN_ORDER,
        cost_estimate=cost(0, 4 * first.nbytes),
        name="turn",
    )(first, second)


def project_kernel(parts, *refs):
    total = dot(refs[0][...], refs[parts][...], 1, 0)
    for part in range(1, parts):
        total += dot(refs[part][...], refs[parts + part][...], 1, 0)
    refs[-1][...] = total.astype(refs[-1].dtype)


def project(turned, grads, first, wide, dtype):
    tokens, columns = grads[0].shape
    tile = min(512, wide)
    skip = first // tile
    return pl.pallas_call(
        functools.partial(project_kernel, len(grads)),
        grid=(wide // tile,),
        in_specs=[pl.BlockSpec((tile, tokens), lambda j: (j + skip, 0))] * len(grads)
        + [pl.BlockSpec((tokens, columns), lambda j: (0, 0))] * len(grads),
        out_specs=pl.BlockSpec((tile, columns), lambda j: (j, 0)),
        out_shape=jax.ShapeDtypeStruct((wide, columns), dtype),
        compiler_params=IN_ORDER,
        cost_estimate=cost(
            2 * len(grads) * wide * tokens * columns,
            len(grads) * (wide * tokens + tokens * columns) * 2,
        ),
        name="project",
    )(*turned, *grads)


def add_kernel(*refs):
    total = refs[0][...].astype(F32)
    for ref in refs[1:-1]:
        total += ref[...].astype(F32)
    refs[-1][...] = total.astype(refs[-1].dtype)


def add_columns(terms, columns):
    wide = terms[0].shape[0]
    tile = min(512, wide)
    return pl.pallas_call(
        add_kernel,
        grid=(wide // tile,),
        in_specs=[pl.BlockSpec((tile, columns), lambda j: (j, 1))] * len(terms),
        out_specs=pl.BlockSpec((tile, columns), lambda j: (j, 0)),
        out_shape=jax.ShapeDtypeStruct((wide, columns), BF16),
        compiler_params=IN_ORDER,
        cost_estimate=cost(0, 8 * len(terms) * wide * columns),
        name="add_columns",
    )(*terms)


def finish_kernel(parts, *refs):
    total = refs[1][...].astype(F32)
    for part in range(1, parts):
        total += refs[1 + part][...].astype(F32)
    refs[-1][...] = jnp.where(refs[0][...] == 1, total, 0.0)


def finish(terms, weight_mask, result, first):
    height, depth = weight_mask.shape
    wide = terms[0].shape[0]
    tile = min(512, wide)
    skip = first // tile
    place = pl.BlockSpec((tile, depth), lambda j: (j + skip, 0))
    in_specs = [place] + [pl.BlockSpec((tile, depth), lambda j: (j, 0))] * len(terms)
    args = [weight_mask, *terms]
    aliases = {}
    if result is not None:
        aliases = {len(args): 0}
        in_specs.append(pl.BlockSpec(memory_space=pl.ANY))
        args.append(result)
    return pl.pallas_call(
        functools.partial(finish_kernel, len(terms)),
        grid=(wide // tile,),
        in_specs=in_specs,
        out_specs=place,
        out_shape=jax.ShapeDtypeStruct((height, depth), F32),
        input_output_aliases=aliases,
        compiler_params=IN_ORDER,
        cost_estimate=cost(0, 16 * wide * depth),
        name="finish",
    )(*args)


def per_device(inputs, queries, keys_values, out_grad, weight_mask, clip_mask):
    depth = keys_values.shape[1]
    rows = inputs.shape[0]
    groups = lax.axis_size("dp")
    chips = lax.axis_size("tensor") // 2
    block = weight_mask.shape[0]
    row_place = lax.axis_index("dp")

    other = swap(keys_values, "tensor", 1)
    mine_rows = []
    for step in range(groups):
        start = (row_place ^ step) * block
        part = lax.dynamic_slice(inputs, (0, start), (rows, block))
        mine_rows.append(part if step == 0 else swap(part, "dp", step))
    turned = [turn(part, swap(part, "tensor", 1)) for part in mine_rows]

    query_grad, mine, theirs = attention(keys_values, other, queries, out_grad)
    arrived = swap(theirs, "tensor", 1)
    blocks = kv_blocks(mine, arrived, clip_mask, rows)

    def gather(steps):
        parts = [blocks[s] if s == 0 else swap(blocks[s], "tensor", 2 * s) for s in steps]
        stacked = jnp.concatenate(parts, 1)
        return [stacked if s == 0 else swap(stacked, "dp", s) for s in range(groups)]

    order = sorted(range(chips), key=lambda s: [(s >> b) & 1 for b in range(8)])
    half = chips // 2
    odd = gather(order[half:])
    even = gather(order[:half])

    cuts = 2 if block % 1024 == 0 else 1
    wide = block // cuts
    sent = [
        swap(project(turned, odd, cut * wide, wide, BF16), "tensor", 2) for cut in range(cuts)
    ]
    weight_grad = None
    for cut in range(cuts):
        terms = [project(turned, even, cut * wide, wide, F32), sent[cut]]
        columns, bit = half * depth, 2
        while columns > depth:
            columns, bit = columns // 2, bit * 2
            terms.append(swap(add_columns(terms, columns), "tensor", bit))
        weight_grad = finish(terms, weight_mask, weight_grad, cut * wide)
    return (query_grad, weight_grad)


def solution(mesh):
    spec = P("dp", "tensor")
    in_specs = (P(("dp", "tensor"), None), spec, spec, spec, spec, spec)
    return jax.shard_map(
        per_device, mesh=mesh, in_specs=in_specs, out_specs=(spec, spec), check_vma=False
    )
```

```python
import functools
import math

import jax
import jax.numpy as jnp
from jax import lax
from jax.experimental import pallas as pl
from jax.experimental.pallas import tpu as pltpu
from jax.sharding import PartitionSpec as P

F32 = jnp.float32
BF16 = jnp.bfloat16
VMEM_LIMIT = 36 * 2**20
IN_ORDER = pltpu.CompilerParams(
    vmem_limit_bytes=VMEM_LIMIT, dimension_semantics=("arbitrary",)
)


def cost(flops, moved, exponents=0):
    return pl.CostEstimate(flops=flops, bytes_accessed=moved, transcendentals=exponents)


def swap(value, axis, mask):
    pairs = [(source, source ^ mask) for source in range(lax.axis_size(axis))]
    return lax.ppermute(value, axis, pairs)


def dot(left, right, left_dim, right_dim):
    dims = (((left_dim,), (right_dim,)), ((), ()))
    return lax.dot_general(left, right, dims, preferred_element_type=F32)


def attention_kernel(height, own_ref, other_ref, q_ref, up_ref, dq_ref, mine_ref, theirs_ref, k_ref, v_ref, dk_ref, dv_ref):
    length, depth = q_ref.shape
    factor = depth**-0.5
    power = factor * math.log2(math.e)
    head = pl.program_id(0)
    is_even = lax.axis_index("tensor") % 2 == 0

    @pl.when(head == 0)
    def _():
        k_ref[...] = jnp.where(is_even, own_ref[...], other_ref[...])
        v_ref[...] = jnp.where(is_even, other_ref[...], own_ref[...])
        dk_ref[...] = jnp.zeros_like(dk_ref)
        dv_ref[...] = jnp.zeros_like(dv_ref)

    half = height // 2
    key_place = lax.broadcasted_iota(jnp.int32, (half, half), 0)
    query_place = lax.broadcasted_iota(jnp.int32, (half, half), 1)
    visible = key_place <= query_place

    def merge(reduce, join, long, short):
        long = reduce(long, axis=0, keepdims=True)
        short = reduce(short, axis=0, keepdims=True)
        return jnp.concatenate([long[:, :half], join(long[:, half:], short)], 1)

    for block in reversed(range(length // height)):
        first = block * height
        middle = first + half
        finish = first + height
        query, upstream = q_ref[first:finish], up_ref[first:finish]
        query_end, upstream_end = query[half:], upstream[half:]
        keys, values = k_ref[:middle], v_ref[:middle]
        keys_end, values_end = k_ref[middle:finish], v_ref[middle:finish]
        scores = dot(keys, query, 1, 1)
        scores_end = dot(keys_end, query_end, 1, 1)
        product = dot(values, upstream, 1, 1)
        product_end = dot(values_end, upstream_end, 1, 1)
        corner = jnp.where(visible, scores[first:, :half], -jnp.inf)
        corner = jnp.concatenate([corner, scores[first:, half:]], 1)
        scores = corner if block == 0 else jnp.concatenate([scores[:first], corner], 0)
        scores_end = jnp.where(visible, scores_end, -jnp.inf)
        biggest = merge(jnp.max, jnp.maximum, scores, scores_end)
        weights = jnp.exp2((scores - biggest) * power)
        weights_end = jnp.exp2((scores_end - biggest[:, half:]) * power)
        scale = 1.0 / merge(jnp.sum, jnp.add, weights, weights_end)
        center = merge(jnp.sum, jnp.add, weights * product, weights_end * product_end) * scale
        weights = weights * scale
        weights_end = weights_end * scale[:, half:]
        grad = (weights * (product - center) * factor).astype(BF16)
        grad_end = (weights_end * (product_end - center[:, half:]) * factor).astype(BF16)
        dv_ref[:middle] += dot(weights.astype(BF16), upstream, 1, 0)
        dv_ref[middle:finish] += dot(weights_end.astype(BF16), upstream_end, 1, 0)
        dk_ref[:middle] += dot(grad, query, 1, 0)
        dk_ref[middle:finish] += dot(grad_end, query_end, 1, 0)
        query_grad = dot(grad, keys, 0, 0)
        dq_ref[first:middle] = query_grad[:half].astype(BF16)
        dq_ref[middle:finish] = (query_grad[half:] + dot(grad_end, keys_end, 0, 0)).astype(BF16)

    @pl.when(head == pl.num_programs(0) - 1)
    def _():
        mine_ref[...] = jnp.where(is_even, dk_ref[...], dv_ref[...])
        theirs_ref[...] = jnp.where(is_even, dv_ref[...], dk_ref[...])


def attention(own, other, queries, out_grad):
    length, width = queries.shape
    depth = own.shape[1]
    height = min(512, length)
    column = pl.BlockSpec((length, depth), lambda h: (0, h))
    whole = pl.BlockSpec((length, depth), lambda h: (0, 0))
    sums = jax.ShapeDtypeStruct((length, depth), F32)
    return pl.pallas_call(
        functools.partial(attention_kernel, height),
        grid=(width // depth,),
        in_specs=[whole, whole, column, column],
        out_specs=[column, whole, whole],
        out_shape=[jax.ShapeDtypeStruct((length, width), BF16), sums, sums],
        scratch_shapes=[
            pltpu.VMEM((length, depth), BF16),
            pltpu.VMEM((length, depth), BF16),
            pltpu.VMEM((length, depth), F32),
            pltpu.VMEM((length, depth), F32),
        ],
        compiler_params=IN_ORDER,
        cost_estimate=cost(
            20 * length * length * width,
            6 * queries.nbytes,
            length * length * width // depth,
        ),
        name="attention",
    )(own, other, queries, out_grad)


def kv_kernel(rows, mine_ref, arrived_ref, mask_ref, *out_refs):
    place = lax.axis_index("tensor")
    chip, core = place // 2, place % 2
    for step, out_ref in enumerate(out_refs):
        for half in range(2):
            start = ((chip ^ step) * 2 + (core ^ half)) * rows
            span = pl.ds(pl.multiple_of(start, rows), rows)
            total = mine_ref[span, :] + arrived_ref[span, :].astype(F32)
            keep = mask_ref[span, :].astype(F32)
            out_ref[half * rows : (half + 1) * rows, :] = (total * keep).astype(BF16)


def kv_blocks(mine, arrived, mask, rows):
    length, depth = mine.shape
    count = length // (2 * rows)
    return pl.pallas_call(
        functools.partial(kv_kernel, rows),
        out_shape=[jax.ShapeDtypeStruct((2 * rows, depth), BF16)] * count,
        compiler_params=pltpu.CompilerParams(vmem_limit_bytes=8 * 2**20),
        cost_estimate=cost(0, 2 * mine.nbytes),
        name="kv_blocks",
    )(mine, arrived, mask)


def per_device(inputs, queries, keys_values, out_grad, weight_mask, clip_mask):
    depth = keys_values.shape[1]
    rows = inputs.shape[0]
    groups = lax.axis_size("dp")
    chips = lax.axis_size("tensor") // 2
    block = weight_mask.shape[0]
    row_place = lax.axis_index("dp")

    other = swap(keys_values, "tensor", 1)
    parts = []
    for step in range(groups):
        start = (row_place ^ step) * block
        part = lax.dynamic_slice(inputs, (0, start), (rows, block))
        parts.append(part if step == 0 else swap(part, "dp", step))

    query_grad, mine, theirs = attention(keys_values, other, queries, out_grad)
    arrived = swap(theirs, "tensor", 1)
    arrived, *parts = lax.optimization_barrier((arrived, *parts))
    pieces = [piece for part in parts for piece in (part, swap(part, "tensor", 1))]
    blocks = kv_blocks(mine, arrived, clip_mask, rows)

    blocks = [b if s == 0 else swap(b, "tensor", 2 * s) for s, b in enumerate(blocks)]
    blocks = lax.optimization_barrier(blocks)
    order = sorted(range(chips), key=lambda s: [(s >> b) & 1 for b in range(8)])
    evens, odds = order[: chips // 2], order[chips // 2 :]

    def gather(steps):
        stacked = jnp.concatenate([blocks[s] for s in steps], 1)
        parts = [stacked if s == 0 else swap(stacked, "dp", s) for s in range(groups)]
        return jnp.concatenate(parts, 0)

    grads_odd = gather(odds)
    grads_even = gather(evens)

    wide = block // 2
    near = jnp.concatenate([p[:, :wide] for p in pieces], 0)
    far = jnp.concatenate([p[:, wide:] for p in pieces], 0)

    def column(step):
        group = evens if step in evens else odds
        place = group.index(step) * depth
        return (grads_even if step in evens else grads_odd)[:, place : place + depth]

    sent = swap(dot(near, grads_odd, 0, 0).astype(BF16), "tensor", 2)
    straight = [
        swap(dot(far, column(step), 0, 0).astype(BF16), "tensor", 2 * step)
        for step in odds + evens[1:]
    ]
    terms = [dot(near, grads_even, 0, 0), sent]
    columns, bit = chips // 2 * depth, 2
    while columns > depth:
        columns, bit = columns // 2, bit * 2
        away = sum(t[:, columns : 2 * columns].astype(F32) for t in terms).astype(BF16)
        terms.append(swap(away, "tensor", bit))
    upper = sum(t[:, :depth].astype(F32) for t in terms)
    lower = dot(far, column(0), 0, 0) + sum(t.astype(F32) for t in straight)
    summed = jnp.concatenate([upper, lower], 0)
    weight_grad = jnp.where(weight_mask == 1, summed, 0.0)
    return (query_grad, weight_grad)


def solution(mesh):
    spec = P("dp", "tensor")
    in_specs = (P(("dp", "tensor"), None), spec, spec, spec, spec, spec)
    return jax.shard_map(
        per_device, mesh=mesh, in_specs=in_specs, out_specs=(spec, spec), check_vma=False
    )
```

```python
import functools
import math

import jax
import jax.numpy as jnp
from jax import lax
from jax.experimental import pallas as pl
from jax.experimental.pallas import tpu as pltpu
from jax.sharding import PartitionSpec as P

F32 = jnp.float32
BF16 = jnp.bfloat16
VMEM_LIMIT = 36 * 2**20
IN_ORDER = pltpu.CompilerParams(
    vmem_limit_bytes=VMEM_LIMIT, dimension_semantics=("arbitrary",)
)


def cost(flops, moved, exponents=0):
    return pl.CostEstimate(flops=flops, bytes_accessed=moved, transcendentals=exponents)


def swap(value, axis, mask):
    pairs = [(source, source ^ mask) for source in range(lax.axis_size(axis))]
    return lax.ppermute(value, axis, pairs)


def dot(left, right, left_dim, right_dim):
    dims = (((left_dim,), (right_dim,)), ((), ()))
    return lax.dot_general(left, right, dims, preferred_element_type=F32)


def attention_kernel(height, own_ref, other_ref, q_ref, up_ref, dq_ref, mine_ref, theirs_ref, k_ref, v_ref, dk_ref, dv_ref):
    length, depth = q_ref.shape
    factor = depth**-0.5
    power = factor * math.log2(math.e)
    head = pl.program_id(0)
    is_even = lax.axis_index("tensor") % 2 == 0

    @pl.when(head == 0)
    def _():
        k_ref[...] = jnp.where(is_even, own_ref[...], other_ref[...])
        v_ref[...] = jnp.where(is_even, other_ref[...], own_ref[...])
        dk_ref[...] = jnp.zeros_like(dk_ref)
        dv_ref[...] = jnp.zeros_like(dv_ref)

    half = height // 2
    key_place = lax.broadcasted_iota(jnp.int32, (half, half), 0)
    query_place = lax.broadcasted_iota(jnp.int32, (half, half), 1)
    visible = key_place <= query_place

    def merge(reduce, join, long, short):
        long = reduce(long, axis=0, keepdims=True)
        short = reduce(short, axis=0, keepdims=True)
        return jnp.concatenate([long[:, :half], join(long[:, half:], short)], 1)

    for block in reversed(range(length // height)):
        first = block * height
        middle = first + half
        finish = first + height
        query, upstream = q_ref[first:finish], up_ref[first:finish]
        query_end, upstream_end = query[half:], upstream[half:]
        keys, values = k_ref[:middle], v_ref[:middle]
        keys_end, values_end = k_ref[middle:finish], v_ref[middle:finish]
        scores = dot(keys, query, 1, 1)
        scores_end = dot(keys_end, query_end, 1, 1)
        product = dot(values, upstream, 1, 1)
        product_end = dot(values_end, upstream_end, 1, 1)
        corner = jnp.where(visible, scores[first:, :half], -jnp.inf)
        corner = jnp.concatenate([corner, scores[first:, half:]], 1)
        scores = corner if block == 0 else jnp.concatenate([scores[:first], corner], 0)
        scores_end = jnp.where(visible, scores_end, -jnp.inf)
        biggest = merge(jnp.max, jnp.maximum, scores, scores_end)
        weights = jnp.exp2((scores - biggest) * power)
        weights_end = jnp.exp2((scores_end - biggest[:, half:]) * power)
        scale = 1.0 / merge(jnp.sum, jnp.add, weights, weights_end)
        center = merge(jnp.sum, jnp.add, weights * product, weights_end * product_end) * scale
        weights = weights * scale
        weights_end = weights_end * scale[:, half:]
        grad = (weights * (product - center) * factor).astype(BF16)
        grad_end = (weights_end * (product_end - center[:, half:]) * factor).astype(BF16)
        dv_ref[:middle] += dot(weights.astype(BF16), upstream, 1, 0)
        dv_ref[middle:finish] += dot(weights_end.astype(BF16), upstream_end, 1, 0)
        dk_ref[:middle] += dot(grad, query, 1, 0)
        dk_ref[middle:finish] += dot(grad_end, query_end, 1, 0)
        query_grad = dot(grad, keys, 0, 0)
        dq_ref[first:middle] = query_grad[:half].astype(BF16)
        dq_ref[middle:finish] = (query_grad[half:] + dot(grad_end, keys_end, 0, 0)).astype(BF16)

    @pl.when(head == pl.num_programs(0) - 1)
    def _():
        mine_ref[...] = jnp.where(is_even, dk_ref[...], dv_ref[...])
        theirs_ref[...] = jnp.where(is_even, dv_ref[...], dk_ref[...])


def attention(own, other, queries, out_grad):
    length, width = queries.shape
    depth = own.shape[1]
    height = min(512, length)
    column = pl.BlockSpec((length, depth), lambda h: (0, h))
    whole = pl.BlockSpec((length, depth), lambda h: (0, 0))
    sums = jax.ShapeDtypeStruct((length, depth), F32)
    return pl.pallas_call(
        functools.partial(attention_kernel, height),
        grid=(width // depth,),
        in_specs=[whole, whole, column, column],
        out_specs=[column, whole, whole],
        out_shape=[jax.ShapeDtypeStruct((length, width), BF16), sums, sums],
        scratch_shapes=[
            pltpu.VMEM((length, depth), BF16),
            pltpu.VMEM((length, depth), BF16),
            pltpu.VMEM((length, depth), F32),
            pltpu.VMEM((length, depth), F32),
        ],
        compiler_params=IN_ORDER,
        cost_estimate=cost(
            20 * length * length * width,
            6 * queries.nbytes,
            length * length * width // depth,
        ),
        name="attention",
    )(own, other, queries, out_grad)


def spread_kernel(plan, source_ref, *refs):
    out_refs, sems = refs[:-1], refs[-1]
    wide = out_refs[0].shape[1]
    place = lax.axis_index("dp")
    copies = []
    for index, (out, first, step, low, high) in enumerate(plan):
        start = pl.multiple_of((place ^ step) * wide, wide)
        copy = pltpu.make_async_copy(
            source_ref.at[low:high, pl.ds(start, wide)],
            out_refs[out].at[first : first + high - low],
            sems.at[index],
        )
        copy.start()
        copies.append(copy)
    for copy in copies:
        copy.wait()


def spread(source, wide, plan):
    heights = {}
    for out, first, _, low, high in plan:
        heights[out] = max(heights.get(out, 0), first + high - low)
    anywhere = pl.BlockSpec(memory_space=pl.ANY)
    return pl.pallas_call(
        functools.partial(spread_kernel, plan),
        in_specs=[anywhere],
        out_specs=[anywhere] * len(heights),
        out_shape=[
            jax.ShapeDtypeStruct((heights[out], wide), source.dtype) for out in sorted(heights)
        ],
        scratch_shapes=[pltpu.SemaphoreType.DMA((len(plan),))],
        cost_estimate=cost(0, 2 * source.nbytes),
        name="spread",
    )(source)


def exchange_rows(inputs, wide):
    rows = inputs.shape[0]
    groups = lax.axis_size("dp")
    if groups != 4:
        parts = spread(inputs, wide, [(s, 0, s, 0, rows) for s in range(groups)])
        return [part if s == 0 else swap(part, "dp", s) for s, part in enumerate(parts)]
    half = rows // 2
    own, left, right = spread(
        inputs,
        wide,
        [(0, 0, 0, 0, rows), (1, 0, 1, 0, rows), (1, rows, 3, 0, half), (2, 0, 2, 0, rows),
         (2, rows, 3, half, rows)],
    )
    left, right = swap(left, "dp", 1), swap(right, "dp", 2)
    upper, lower = swap(left[rows:], "dp", 2), swap(right[rows:], "dp", 1)
    return [own, left[:rows], right[:rows], jnp.concatenate([upper, lower], 0)]


def kv_kernel(rows, mine_ref, arrived_ref, mask_ref, *out_refs):
    place = lax.axis_index("tensor")
    chip, core = place // 2, place % 2
    for step, out_ref in enumerate(out_refs):
        for half in range(2):
            start = ((chip ^ step) * 2 + (core ^ half)) * rows
            span = pl.ds(pl.multiple_of(start, rows), rows)
            total = mine_ref[span, :] + arrived_ref[span, :].astype(F32)
            keep = mask_ref[span, :].astype(F32)
            out_ref[half * rows : (half + 1) * rows, :] = (total * keep).astype(BF16)


def kv_blocks(mine, arrived, mask, rows):
    length, depth = mine.shape
    count = length // (2 * rows)
    return pl.pallas_call(
        functools.partial(kv_kernel, rows),
        out_shape=[jax.ShapeDtypeStruct((2 * rows, depth), BF16)] * count,
        compiler_params=pltpu.CompilerParams(vmem_limit_bytes=8 * 2**20),
        cost_estimate=cost(0, 2 * mine.nbytes),
        name="kv_blocks",
    )(mine, arrived, mask)


def per_device(inputs, queries, keys_values, out_grad, weight_mask, clip_mask):
    depth = keys_values.shape[1]
    rows = inputs.shape[0]
    groups = lax.axis_size("dp")
    chips = lax.axis_size("tensor") // 2
    block = weight_mask.shape[0]

    other = swap(keys_values, "tensor", 1)
    parts = exchange_rows(inputs, block)
    query_grad, mine, theirs = attention(keys_values, other, queries, out_grad)
    arrived = swap(theirs, "tensor", 1)
    blocks = kv_blocks(mine, arrived, clip_mask, rows)

    blocks = [b if s == 0 else swap(b, "tensor", 2 * s) for s, b in enumerate(blocks)]
    blocks, parts = lax.optimization_barrier((blocks, parts))
    order = sorted(range(chips), key=lambda s: [(s >> b) & 1 for b in range(8)])
    evens, odds = order[: chips // 2], order[chips // 2 :]

    def gather(stacked):
        found = [stacked if s == 0 else swap(stacked, "dp", s) for s in range(groups)]
        return [jnp.concatenate([f[h * rows : (h + 1) * rows] for f in found], 0) for h in (0, 1)]

    wide = block // 2
    cuts = []
    for cut in range(2):
        own = jnp.concatenate([p[:, cut * wide : (cut + 1) * wide] for p in parts], 0)
        cuts.append((own, swap(own, "tensor", 1)))
    near, far = cuts

    def product(pair, grads, place=None):
        if place is not None:
            grads = [g[:, place * depth : (place + 1) * depth] for g in grads]
        return dot(pair[0], grads[0], 0, 0) + dot(pair[1], grads[1], 0, 0)

    def send(value, step):
        return swap(value.astype(BF16), "tensor", 2 * step)

    grads = gather(jnp.concatenate([blocks[s] for s in order], 1))
    half = chips // 2 * depth
    even, odd = [g[:, :half] for g in grads], [g[:, half:] for g in grads]
    sent = send(product(near, odd), 1)
    late = {s: product(far, odd, odds.index(s)).astype(BF16) for s in odds}
    late.update({s: product(far, even, evens.index(s)).astype(BF16) for s in evens[1:]})
    straight = [send(late[s], s) for s in range(2, chips)]
    nearest, straight = lax.optimization_barrier((late[1], straight))
    terms = [product(near, even), sent]
    columns, bit = chips // 2 * depth, 1
    while columns > depth:
        columns, bit = columns // 2, bit * 2
        terms.append(send(sum(t[:, columns : 2 * columns].astype(F32) for t in terms), bit))
    straight.append(send(nearest, 1))
    upper = sum(t[:, :depth].astype(F32) for t in terms)
    lower = product(far, even, 0) + sum(t.astype(F32) for t in straight)
    summed = jnp.concatenate([upper, lower], 0)
    weight_grad = jnp.where(weight_mask == 1, summed, 0.0)
    return (query_grad, weight_grad)


def solution(mesh):
    spec = P("dp", "tensor")
    in_specs = (P(("dp", "tensor"), None), spec, spec, spec, spec, spec)
    return jax.shard_map(
        per_device, mesh=mesh, in_specs=in_specs, out_specs=(spec, spec), check_vma=False
    )
```

```python
import functools
import math

import jax
import jax.numpy as jnp
from jax import lax
from jax.experimental import pallas as pl
from jax.experimental.pallas import tpu as pltpu
from jax.sharding import PartitionSpec as P

F32 = jnp.float32
BF16 = jnp.bfloat16
VMEM_LIMIT = 36 * 2**20
IN_ORDER = pltpu.CompilerParams(
    vmem_limit_bytes=VMEM_LIMIT, dimension_semantics=("arbitrary",)
)


def cost(flops, moved, exponents=0):
    return pl.CostEstimate(flops=flops, bytes_accessed=moved, transcendentals=exponents)


def swap(value, axis, mask):
    pairs = [(source, source ^ mask) for source in range(lax.axis_size(axis))]
    return lax.ppermute(value, axis, pairs)


def dot(left, right, left_dim, right_dim):
    dims = (((left_dim,), (right_dim,)), ((), ()))
    return lax.dot_general(left, right, dims, preferred_element_type=F32)


def attention_kernel(height, own_ref, other_ref, q_ref, up_ref, dq_ref, mine_ref, theirs_ref, k_ref, v_ref, dk_ref, dv_ref):
    length, depth = q_ref.shape
    factor = depth**-0.5
    power = factor * math.log2(math.e)
    head = pl.program_id(0)
    is_even = lax.axis_index("tensor") % 2 == 0

    @pl.when(head == 0)
    def _():
        k_ref[...] = jnp.where(is_even, own_ref[...], other_ref[...])
        v_ref[...] = jnp.where(is_even, other_ref[...], own_ref[...])
        dk_ref[...] = jnp.zeros_like(dk_ref)
        dv_ref[...] = jnp.zeros_like(dv_ref)

    half = height // 2
    key_place = lax.broadcasted_iota(jnp.int32, (half, half), 0)
    query_place = lax.broadcasted_iota(jnp.int32, (half, half), 1)
    visible = key_place <= query_place

    def merge(reduce, join, long, short):
        long = reduce(long, axis=0, keepdims=True)
        short = reduce(short, axis=0, keepdims=True)
        return jnp.concatenate([long[:, :half], join(long[:, half:], short)], 1)

    for block in reversed(range(length // height)):
        first = block * height
        middle = first + half
        finish = first + height
        query, upstream = q_ref[first:finish], up_ref[first:finish]
        query_end, upstream_end = query[half:], upstream[half:]
        keys, values = k_ref[:middle], v_ref[:middle]
        keys_end, values_end = k_ref[middle:finish], v_ref[middle:finish]
        scores = dot(keys, query, 1, 1)
        scores_end = dot(keys_end, query_end, 1, 1)
        product = dot(values, upstream, 1, 1)
        product_end = dot(values_end, upstream_end, 1, 1)
        corner = jnp.where(visible, scores[first:, :half], -jnp.inf)
        corner = jnp.concatenate([corner, scores[first:, half:]], 1)
        scores = corner if block == 0 else jnp.concatenate([scores[:first], corner], 0)
        scores_end = jnp.where(visible, scores_end, -jnp.inf)
        biggest = merge(jnp.max, jnp.maximum, scores, scores_end)
        weights = jnp.exp2((scores - biggest) * power)
        weights_end = jnp.exp2((scores_end - biggest[:, half:]) * power)
        scale = 1.0 / merge(jnp.sum, jnp.add, weights, weights_end)
        center = merge(jnp.sum, jnp.add, weights * product, weights_end * product_end) * scale
        weights = weights * scale
        weights_end = weights_end * scale[:, half:]
        grad = (weights * (product - center) * factor).astype(BF16)
        grad_end = (weights_end * (product_end - center[:, half:]) * factor).astype(BF16)
        dv_ref[:middle] += dot(weights.astype(BF16), upstream, 1, 0)
        dv_ref[middle:finish] += dot(weights_end.astype(BF16), upstream_end, 1, 0)
        dk_ref[:middle] += dot(grad, query, 1, 0)
        dk_ref[middle:finish] += dot(grad_end, query_end, 1, 0)
        query_grad = dot(grad, keys, 0, 0)
        dq_ref[first:middle] = query_grad[:half].astype(BF16)
        dq_ref[middle:finish] = (query_grad[half:] + dot(grad_end, keys_end, 0, 0)).astype(BF16)

    @pl.when(head == pl.num_programs(0) - 1)
    def _():
        mine_ref[...] = jnp.where(is_even, dk_ref[...], dv_ref[...])
        theirs_ref[...] = jnp.where(is_even, dv_ref[...], dk_ref[...])


def attention(own, other, queries, out_grad):
    length, width = queries.shape
    depth = own.shape[1]
    height = min(512, length)
    column = pl.BlockSpec((length, depth), lambda h: (0, h))
    whole = pl.BlockSpec((length, depth), lambda h: (0, 0))
    sums = jax.ShapeDtypeStruct((length, depth), F32)
    return pl.pallas_call(
        functools.partial(attention_kernel, height),
        grid=(width // depth,),
        in_specs=[whole, whole, column, column],
        out_specs=[column, whole, whole],
        out_shape=[jax.ShapeDtypeStruct((length, width), BF16), sums, sums],
        scratch_shapes=[
            pltpu.VMEM((length, depth), BF16),
            pltpu.VMEM((length, depth), BF16),
            pltpu.VMEM((length, depth), F32),
            pltpu.VMEM((length, depth), F32),
        ],
        compiler_params=IN_ORDER,
        cost_estimate=cost(
            20 * length * length * width,
            6 * queries.nbytes,
            length * length * width // depth,
        ),
        name="attention",
    )(own, other, queries, out_grad)


def spread_kernel(plan, source_ref, *out_refs):
    wide = out_refs[0].shape[1]
    place = lax.axis_index("dp")
    for out, first, step, low, high in plan:
        start = pl.multiple_of((place ^ step) * wide, wide)
        out_refs[out][first : first + high - low] = source_ref[low:high, pl.ds(start, wide)]


def spread(source, wide, plan):
    heights = {}
    for out, first, _, low, high in plan:
        heights[out] = max(heights.get(out, 0), first + high - low)
    return pl.pallas_call(
        functools.partial(spread_kernel, plan),
        out_shape=[
            jax.ShapeDtypeStruct((heights[out], wide), source.dtype) for out in sorted(heights)
        ],
        compiler_params=pltpu.CompilerParams(vmem_limit_bytes=16 * 2**20),
        cost_estimate=cost(0, 2 * source.nbytes),
        name="spread",
    )(source)


def exchange_rows(inputs, wide):
    rows = inputs.shape[0]
    groups = lax.axis_size("dp")
    if groups != 4:
        parts = spread(inputs, wide, [(s, 0, s, 0, rows) for s in range(groups)])
        return [part if s == 0 else swap(part, "dp", s) for s, part in enumerate(parts)]
    half = rows // 2
    own, left, right = spread(
        inputs,
        wide,
        [(0, 0, 0, 0, rows), (1, 0, 1, 0, rows), (1, rows, 3, 0, half), (2, 0, 2, 0, rows),
         (2, rows, 3, half, rows)],
    )
    left, right = swap(left, "dp", 1), swap(right, "dp", 2)
    upper, lower = swap(left[rows:], "dp", 2), swap(right[rows:], "dp", 1)
    return [own, left[:rows], right[:rows], jnp.concatenate([upper, lower], 0)]


def kv_kernel(rows, mine_ref, arrived_ref, mask_ref, *out_refs):
    place = lax.axis_index("tensor")
    chip, core = place // 2, place % 2
    for step, out_ref in enumerate(out_refs):
        for half in range(2):
            start = ((chip ^ step) * 2 + (core ^ half)) * rows
            span = pl.ds(pl.multiple_of(start, rows), rows)
            total = mine_ref[span, :] + arrived_ref[span, :].astype(F32)
            keep = mask_ref[span, :].astype(F32)
            out_ref[half * rows : (half + 1) * rows, :] = (total * keep).astype(BF16)


def kv_blocks(mine, arrived, mask, rows):
    length, depth = mine.shape
    count = length // (2 * rows)
    return pl.pallas_call(
        functools.partial(kv_kernel, rows),
        out_shape=[jax.ShapeDtypeStruct((2 * rows, depth), BF16)] * count,
        compiler_params=pltpu.CompilerParams(vmem_limit_bytes=8 * 2**20),
        cost_estimate=cost(0, 2 * mine.nbytes),
        name="kv_blocks",
    )(mine, arrived, mask)


def per_device(inputs, queries, keys_values, out_grad, weight_mask, clip_mask):
    depth = keys_values.shape[1]
    rows = inputs.shape[0]
    groups = lax.axis_size("dp")
    chips = lax.axis_size("tensor") // 2
    block = weight_mask.shape[0]

    other = swap(keys_values, "tensor", 1)
    parts = exchange_rows(inputs, block)
    query_grad, mine, theirs = attention(keys_values, other, queries, out_grad)
    arrived = swap(theirs, "tensor", 1)
    blocks = kv_blocks(mine, arrived, clip_mask, rows)

    blocks = [b if s == 0 else swap(b, "tensor", 2 * s) for s, b in enumerate(blocks)]
    blocks, parts = lax.optimization_barrier((blocks, parts))
    order = sorted(range(chips), key=lambda s: [(s >> b) & 1 for b in range(8)])
    evens, odds = order[: chips // 2], order[chips // 2 :]

    def gather(stacked):
        found = [stacked if s == 0 else swap(stacked, "dp", s) for s in range(groups)]
        return [jnp.concatenate([f[h * rows : (h + 1) * rows] for f in found], 0) for h in (0, 1)]

    wide = block // 2
    cuts = []
    for cut in range(2):
        own = jnp.concatenate([p[:, cut * wide : (cut + 1) * wide] for p in parts], 0)
        cuts.append((own, swap(own, "tensor", 1)))
    near, far = cuts

    def product(pair, grads, place=None):
        if place is not None:
            grads = [g[:, place * depth : (place + 1) * depth] for g in grads]
        return dot(pair[0], grads[0], 0, 0) + dot(pair[1], grads[1], 0, 0)

    def send(value, step):
        return swap(value.astype(BF16), "tensor", 2 * step)

    grads = gather(jnp.concatenate([blocks[s] for s in order], 1))
    half = chips // 2 * depth
    even, odd = [g[:, :half] for g in grads], [g[:, half:] for g in grads]
    sent = send(product(near, odd), 1)
    late = {s: product(far, odd, odds.index(s)).astype(BF16) for s in odds}
    late.update({s: product(far, even, evens.index(s)).astype(BF16) for s in evens[1:]})
    straight = [send(late[s], s) for s in range(2, chips)]
    terms = [product(near, even), sent]
    columns, bit = half, 1
    while columns > depth:
        columns, bit = columns // 2, bit * 2
        away = sum(t[:, columns : 2 * columns].astype(F32) for t in terms).astype(BF16)
        terms.append(send(away, bit))
    nearest, straight, _ = lax.optimization_barrier((late[1], straight, away))
    straight.append(send(nearest, 1))
    upper = sum(t[:, :depth].astype(F32) for t in terms)
    lower = product(far, even, 0) + sum(t.astype(F32) for t in straight)
    summed = jnp.concatenate([upper, lower], 0)
    weight_grad = jnp.where(weight_mask == 1, summed, 0.0)
    return (query_grad, weight_grad)


def solution(mesh):
    spec = P("dp", "tensor")
    in_specs = (P(("dp", "tensor"), None), spec, spec, spec, spec, spec)
    return jax.shard_map(
        per_device, mesh=mesh, in_specs=in_specs, out_specs=(spec, spec), check_vma=False
    )
```

```python
import functools
import math

import jax
import jax.numpy as jnp
from jax import lax
from jax.experimental import pallas as pl
from jax.experimental.pallas import tpu as pltpu
from jax.sharding import PartitionSpec as P

F32 = jnp.float32
BF16 = jnp.bfloat16
VMEM_LIMIT = 50 * 2**20
IN_ORDER = pltpu.CompilerParams(
    vmem_limit_bytes=VMEM_LIMIT, dimension_semantics=("arbitrary",)
)


def cost(flops, moved, exponents=0):
    return pl.CostEstimate(flops=flops, bytes_accessed=moved, transcendentals=exponents)


def swap(value, axis, mask):
    pairs = [(source, source ^ mask) for source in range(lax.axis_size(axis))]
    return lax.ppermute(value, axis, pairs)


def dot(left, right, left_dim, right_dim):
    dims = (((left_dim,), (right_dim,)), ((), ()))
    return lax.dot_general(left, right, dims, preferred_element_type=F32)


def attention_kernel(height, own_ref, other_ref, q_ref, up_ref, dq_ref, mine_ref, theirs_ref, k_ref, v_ref, dk_ref, dv_ref):
    length, depth = q_ref.shape
    factor = depth**-0.5
    power = factor * math.log2(math.e)
    head = pl.program_id(0)
    is_even = lax.axis_index("tensor") % 2 == 0

    @pl.when(head == 0)
    def _():
        k_ref[...] = jnp.where(is_even, own_ref[...], other_ref[...])
        v_ref[...] = jnp.where(is_even, other_ref[...], own_ref[...])
        dk_ref[...] = jnp.zeros_like(dk_ref)
        dv_ref[...] = jnp.zeros_like(dv_ref)

    half = height // 2
    key_place = lax.broadcasted_iota(jnp.int32, (half, half), 0)
    query_place = lax.broadcasted_iota(jnp.int32, (half, half), 1)
    visible = key_place <= query_place

    def merge(reduce, join, long, short):
        long = reduce(long, axis=0, keepdims=True)
        short = reduce(short, axis=0, keepdims=True)
        return jnp.concatenate([long[:, :half], join(long[:, half:], short)], 1)

    for block in reversed(range(length // height)):
        first = block * height
        middle = first + half
        finish = first + height
        query, upstream = q_ref[first:finish], up_ref[first:finish]
        query_end, upstream_end = query[half:], upstream[half:]
        keys, values = k_ref[:middle], v_ref[:middle]
        keys_end, values_end = k_ref[middle:finish], v_ref[middle:finish]
        scores = dot(keys, query, 1, 1)
        scores_end = dot(keys_end, query_end, 1, 1)
        product = dot(values, upstream, 1, 1)
        product_end = dot(values_end, upstream_end, 1, 1)
        corner = jnp.where(visible, scores[first:, :half], -jnp.inf)
        corner = jnp.concatenate([corner, scores[first:, half:]], 1)
        scores = corner if block == 0 else jnp.concatenate([scores[:first], corner], 0)
        scores_end = jnp.where(visible, scores_end, -jnp.inf)
        biggest = merge(jnp.max, jnp.maximum, scores, scores_end)
        weights = jnp.exp2((scores - biggest) * power)
        weights_end = jnp.exp2((scores_end - biggest[:, half:]) * power)
        scale = 1.0 / merge(jnp.sum, jnp.add, weights, weights_end)
        center = merge(jnp.sum, jnp.add, weights * product, weights_end * product_end) * scale
        weights = weights * scale
        weights_end = weights_end * scale[:, half:]
        grad = (weights * (product - center) * factor).astype(BF16)
        grad_end = (weights_end * (product_end - center[:, half:]) * factor).astype(BF16)
        dv_ref[:middle] += dot(weights.astype(BF16), upstream, 1, 0)
        dv_ref[middle:finish] += dot(weights_end.astype(BF16), upstream_end, 1, 0)
        dk_ref[:middle] += dot(grad, query, 1, 0)
        dk_ref[middle:finish] += dot(grad_end, query_end, 1, 0)
        query_grad = dot(grad, keys, 0, 0)
        dq_ref[first:middle] = query_grad[:half].astype(BF16)
        dq_ref[middle:finish] = (query_grad[half:] + dot(grad_end, keys_end, 0, 0)).astype(BF16)

    @pl.when(head == pl.num_programs(0) - 1)
    def _():
        mine_ref[...] = jnp.where(is_even, dk_ref[...], dv_ref[...])
        theirs_ref[...] = jnp.where(is_even, dv_ref[...], dk_ref[...])


def attention(own, other, queries, out_grad):
    length, width = queries.shape
    depth = own.shape[1]
    height = min(512, length)
    column = pl.BlockSpec((length, depth), lambda h: (0, h))
    whole = pl.BlockSpec((length, depth), lambda h: (0, 0))
    sums = jax.ShapeDtypeStruct((length, depth), F32)
    return pl.pallas_call(
        functools.partial(attention_kernel, height),
        grid=(width // depth,),
        in_specs=[whole, whole, column, column],
        out_specs=[column, whole, whole],
        out_shape=[jax.ShapeDtypeStruct((length, width), BF16), sums, sums],
        scratch_shapes=[
            pltpu.VMEM((length, depth), BF16),
            pltpu.VMEM((length, depth), BF16),
            pltpu.VMEM((length, depth), F32),
            pltpu.VMEM((length, depth), F32),
        ],
        compiler_params=IN_ORDER,
        cost_estimate=cost(
            20 * length * length * width,
            6 * queries.nbytes,
            length * length * width // depth,
        ),
        name="attention",
    )(own, other, queries, out_grad)


def spread_kernel(plan, source_ref, *out_refs):
    wide = out_refs[0].shape[1]
    place = lax.axis_index("dp")
    for out, first, step, low, high in plan:
        start = pl.multiple_of((place ^ step) * wide, wide)
        out_refs[out][first : first + high - low] = source_ref[low:high, pl.ds(start, wide)]


def spread(source, wide, plan):
    heights = {}
    for out, first, _, low, high in plan:
        heights[out] = max(heights.get(out, 0), first + high - low)
    return pl.pallas_call(
        functools.partial(spread_kernel, plan),
        out_shape=[
            jax.ShapeDtypeStruct((heights[out], wide), source.dtype) for out in sorted(heights)
        ],
        compiler_params=pltpu.CompilerParams(vmem_limit_bytes=16 * 2**20),
        cost_estimate=cost(0, 2 * source.nbytes),
        name="spread",
    )(source)


def exchange_rows(inputs, wide):
    rows = inputs.shape[0]
    groups = lax.axis_size("dp")
    if groups != 4:
        parts = spread(inputs, wide, [(s, 0, s, 0, rows) for s in range(groups)])
        return [part if s == 0 else swap(part, "dp", s) for s, part in enumerate(parts)]
    half = rows // 2
    own, left, right = spread(
        inputs,
        wide,
        [(0, 0, 0, 0, rows), (1, 0, 1, 0, rows), (1, rows, 3, 0, half), (2, 0, 2, 0, rows),
         (2, rows, 3, half, rows)],
    )
    left, right = swap(left, "dp", 1), swap(right, "dp", 2)
    upper, lower = swap(left[rows:], "dp", 2), swap(right[rows:], "dp", 1)
    return [own, left[:rows], right[:rows], jnp.concatenate([upper, lower], 0)]


def kv_kernel(rows, mine_ref, arrived_ref, mask_ref, *out_refs):
    place = lax.axis_index("tensor")
    chip, core = place // 2, place % 2
    for step, out_ref in enumerate(out_refs):
        for half in range(2):
            start = ((chip ^ step) * 2 + (core ^ half)) * rows
            span = pl.ds(pl.multiple_of(start, rows), rows)
            total = mine_ref[span, :] + arrived_ref[span, :].astype(F32)
            keep = mask_ref[span, :].astype(F32)
            out_ref[half * rows : (half + 1) * rows, :] = (total * keep).astype(BF16)


def kv_blocks(mine, arrived, mask, rows):
    length, depth = mine.shape
    count = length // (2 * rows)
    return pl.pallas_call(
        functools.partial(kv_kernel, rows),
        out_shape=[jax.ShapeDtypeStruct((2 * rows, depth), BF16)] * count,
        compiler_params=pltpu.CompilerParams(vmem_limit_bytes=8 * 2**20),
        cost_estimate=cost(0, 2 * mine.nbytes),
        name="kv_blocks",
    )(mine, arrived, mask)


def per_device(inputs, queries, keys_values, out_grad, weight_mask, clip_mask):
    depth = keys_values.shape[1]
    rows = inputs.shape[0]
    groups = lax.axis_size("dp")
    chips = lax.axis_size("tensor") // 2
    block = weight_mask.shape[0]

    other = swap(keys_values, "tensor", 1)
    parts = exchange_rows(inputs, block)
    query_grad, mine, theirs = attention(keys_values, other, queries, out_grad)
    arrived = swap(theirs, "tensor", 1)
    blocks = kv_blocks(mine, arrived, clip_mask, rows)

    blocks = [b if s == 0 else swap(b, "tensor", 2 * s) for s, b in enumerate(blocks)]
    blocks[-1], parts = lax.optimization_barrier((blocks[-1], parts))
    order = sorted(range(chips), key=lambda s: [(s >> b) & 1 for b in range(8)])
    evens, odds = order[: chips // 2], order[chips // 2 :]

    groups_of = (range(chips // 2), range(chips // 2, chips))
    found = []
    for steps in groups_of:
        stacked = jnp.concatenate([blocks[s] for s in steps], 1)
        found.append([stacked if s == 0 else swap(stacked, "dp", s) for s in range(groups)])
    found = lax.optimization_barrier(found)
    grads = [None] * chips
    for steps, group in zip(groups_of, found):
        for place, step in enumerate(steps):
            columns = slice(place * depth, (place + 1) * depth)
            grads[step] = [
                jnp.concatenate([f[h * rows : (h + 1) * rows, columns] for f in group], 0)
                for h in (0, 1)
            ]

    wide = block // 2
    cuts = []
    for cut in range(2):
        own = jnp.concatenate([p[:, cut * wide : (cut + 1) * wide] for p in parts], 0)
        cuts.append((own, swap(own, "tensor", 1)))
    near, far = cuts

    def product(pair, grads):
        return dot(pair[0], grads[0], 0, 0) + dot(pair[1], grads[1], 0, 0)

    def send(value, step):
        return swap(value.astype(BF16), "tensor", 2 * step)

    def joined(steps):
        return [jnp.concatenate([grads[s][h] for s in steps], 1) for h in (0, 1)]

    odd, even = joined(odds), joined(evens)
    straight = [send(product(far, grads[s]), s) for s in range(2, chips)]
    sent = send(product(near, odd), 1)
    sent, straight = lax.optimization_barrier((sent, straight))
    terms = [product(near, even), sent]
    columns, bit = chips // 2 * depth, 1
    while columns > depth:
        columns, bit = columns // 2, bit * 2
        away = sum(t[:, columns : 2 * columns].astype(F32) for t in terms).astype(BF16)
        terms.append(send(away, bit))
    nearest, _ = lax.optimization_barrier((product(far, grads[1]).astype(BF16), away))
    straight.append(send(nearest, 1))
    upper = sum(t[:, :depth].astype(F32) for t in terms)
    lower = product(far, grads[0]) + sum(t.astype(F32) for t in straight)
    summed = jnp.concatenate([upper, lower], 0)
    weight_grad = jnp.where(weight_mask == 1, summed, 0.0)
    return (query_grad, weight_grad)


def solution(mesh):
    spec = P("dp", "tensor")
    in_specs = (P(("dp", "tensor"), None), spec, spec, spec, spec, spec)
    return jax.shard_map(
        per_device, mesh=mesh, in_specs=in_specs, out_specs=(spec, spec), check_vma=False
    )
```

```python
import functools
import math

import jax
import jax.numpy as jnp
from jax import lax
from jax.experimental import pallas as pl
from jax.experimental.pallas import tpu as pltpu
from jax.sharding import PartitionSpec as P

F32 = jnp.float32
BF16 = jnp.bfloat16
VMEM_LIMIT = 50 * 2**20
IN_ORDER = pltpu.CompilerParams(
    vmem_limit_bytes=VMEM_LIMIT, dimension_semantics=("arbitrary",)
)


SMALL = pltpu.CompilerParams(vmem_limit_bytes=16 * 2**20)


def cost(flops, moved, exponents=0):
    return pl.CostEstimate(flops=flops, bytes_accessed=moved, transcendentals=exponents)


def swap(value, axis, mask):
    pairs = [(source, source ^ mask) for source in range(lax.axis_size(axis))]
    return lax.ppermute(value, axis, pairs)


def dot(left, right, left_dim, right_dim):
    dims = (((left_dim,), (right_dim,)), ((), ()))
    return lax.dot_general(left, right, dims, preferred_element_type=F32)


def attention_kernel(height, own_ref, other_ref, q_ref, up_ref, dq_ref, mine_ref, theirs_ref, k_ref, v_ref, dk_ref, dv_ref):
    length, depth = q_ref.shape
    factor = depth**-0.5
    power = factor * math.log2(math.e)
    head = pl.program_id(0)
    is_even = lax.axis_index("tensor") % 2 == 0

    @pl.when(head == 0)
    def _():
        k_ref[...] = jnp.where(is_even, own_ref[...], other_ref[...])
        v_ref[...] = jnp.where(is_even, other_ref[...], own_ref[...])
        dk_ref[...] = jnp.zeros_like(dk_ref)
        dv_ref[...] = jnp.zeros_like(dv_ref)

    half = height // 2
    key_place = lax.broadcasted_iota(jnp.int32, (half, half), 0)
    query_place = lax.broadcasted_iota(jnp.int32, (half, half), 1)
    visible = key_place <= query_place

    def merge(reduce, join, long, short):
        long = reduce(long, axis=0, keepdims=True)
        short = reduce(short, axis=0, keepdims=True)
        return jnp.concatenate([long[:, :half], join(long[:, half:], short)], 1)

    for block in reversed(range(length // height)):
        first = block * height
        middle = first + half
        finish = first + height
        query, upstream = q_ref[first:finish], up_ref[first:finish]
        query_end, upstream_end = query[half:], upstream[half:]
        keys, values = k_ref[:middle], v_ref[:middle]
        keys_end, values_end = k_ref[middle:finish], v_ref[middle:finish]
        scores = dot(keys, query, 1, 1)
        scores_end = dot(keys_end, query_end, 1, 1)
        product = dot(values, upstream, 1, 1)
        product_end = dot(values_end, upstream_end, 1, 1)
        corner = jnp.where(visible, scores[first:, :half], -jnp.inf)
        corner = jnp.concatenate([corner, scores[first:, half:]], 1)
        scores = corner if block == 0 else jnp.concatenate([scores[:first], corner], 0)
        scores_end = jnp.where(visible, scores_end, -jnp.inf)
        biggest = merge(jnp.max, jnp.maximum, scores, scores_end)
        weights = jnp.exp2((scores - biggest) * power)
        weights_end = jnp.exp2((scores_end - biggest[:, half:]) * power)
        scale = 1.0 / merge(jnp.sum, jnp.add, weights, weights_end)
        center = merge(jnp.sum, jnp.add, weights * product, weights_end * product_end) * scale
        weights = weights * scale
        weights_end = weights_end * scale[:, half:]
        grad = (weights * (product - center) * factor).astype(BF16)
        grad_end = (weights_end * (product_end - center[:, half:]) * factor).astype(BF16)
        dv_ref[:middle] += dot(weights.astype(BF16), upstream, 1, 0)
        dv_ref[middle:finish] += dot(weights_end.astype(BF16), upstream_end, 1, 0)
        dk_ref[:middle] += dot(grad, query, 1, 0)
        dk_ref[middle:finish] += dot(grad_end, query_end, 1, 0)
        query_grad = dot(grad, keys, 0, 0)
        dq_ref[first:middle] = query_grad[:half].astype(BF16)
        dq_ref[middle:finish] = (query_grad[half:] + dot(grad_end, keys_end, 0, 0)).astype(BF16)

    @pl.when(head == pl.num_programs(0) - 1)
    def _():
        mine_ref[...] = jnp.where(is_even, dk_ref[...], dv_ref[...])
        theirs_ref[...] = jnp.where(is_even, dv_ref[...], dk_ref[...])


def attention(own, other, queries, out_grad):
    length, width = queries.shape
    depth = own.shape[1]
    height = min(512, length)
    column = pl.BlockSpec((length, depth), lambda h: (0, h))
    whole = pl.BlockSpec((length, depth), lambda h: (0, 0))
    sums = jax.ShapeDtypeStruct((length, depth), F32)
    return pl.pallas_call(
        functools.partial(attention_kernel, height),
        grid=(width // depth,),
        in_specs=[whole, whole, column, column],
        out_specs=[column, whole, whole],
        out_shape=[jax.ShapeDtypeStruct((length, width), BF16), sums, sums],
        scratch_shapes=[
            pltpu.VMEM((length, depth), BF16),
            pltpu.VMEM((length, depth), BF16),
            pltpu.VMEM((length, depth), F32),
            pltpu.VMEM((length, depth), F32),
        ],
        compiler_params=IN_ORDER,
        cost_estimate=cost(
            20 * length * length * width,
            6 * queries.nbytes,
            length * length * width // depth,
        ),
        name="attention",
    )(own, other, queries, out_grad)


def spread_kernel(plan, source_ref, *out_refs):
    wide = out_refs[0].shape[1]
    place = lax.axis_index("dp")
    for out, first, step, low, high in plan:
        start = pl.multiple_of((place ^ step) * wide, wide)
        out_refs[out][first : first + high - low] = source_ref[low:high, pl.ds(start, wide)]


def spread(source, wide, plan):
    heights = {}
    for out, first, _, low, high in plan:
        heights[out] = max(heights.get(out, 0), first + high - low)
    return pl.pallas_call(
        functools.partial(spread_kernel, plan),
        out_shape=[
            jax.ShapeDtypeStruct((heights[out], wide), source.dtype) for out in sorted(heights)
        ],
        compiler_params=SMALL,
        cost_estimate=cost(0, 2 * source.nbytes),
        name="spread",
    )(source)


def lay(sources, outputs):
    def kernel(*refs):
        for out_ref, (_, entries) in zip(refs[len(sources) :], outputs):
            for source, rows, columns, first in entries:
                height = rows.stop - rows.start
                out_ref[first : first + height] = refs[source][rows, columns]

    moved = sum(2 * math.prod(shape) * 2 for shape, _ in outputs)
    return pl.pallas_call(
        kernel,
        out_shape=[jax.ShapeDtypeStruct(shape, sources[0].dtype) for shape, _ in outputs],
        compiler_params=SMALL,
        cost_estimate=cost(0, moved),
        name="lay",
    )(*sources)


def send_rows(inputs, wide):
    rows = inputs.shape[0]
    groups = lax.axis_size("dp")
    if groups != 4:
        parts = spread(inputs, wide, [(s, 0, s, 0, rows) for s in range(groups)])
        return [part if s == 0 else swap(part, "dp", s) for s, part in enumerate(parts)]
    half = rows // 2
    own, left, right = spread(
        inputs,
        wide,
        [(0, 0, 0, 0, rows), (1, 0, 1, 0, rows), (1, rows, 3, 0, half), (2, 0, 2, 0, rows),
         (2, rows, 3, half, rows)],
    )
    return [own, swap(left, "dp", 1), swap(right, "dp", 2)]


def pass_rows(parts, wide):
    rows = parts[0].shape[0]
    groups = lax.axis_size("dp")
    if groups != 4:
        return parts, [[(s, slice(0, rows))] for s in range(groups)]
    own, left, right = parts
    half = rows // 2
    tail = slice(rows, rows + half)
    every = slice(None)
    upper, lower = lay(
        [left, right],
        [((half, wide), [(0, tail, every, 0)]), ((half, wide), [(1, tail, every, 0)])],
    )
    upper, lower = swap(upper, "dp", 2), swap(lower, "dp", 1)
    whole, part = slice(0, rows), slice(0, half)
    places = [[(0, whole)], [(1, whole)], [(2, whole)], [(3, part), (4, part)]]
    return [own, left, right, upper, lower], places


def product_kernel(jobs, depth, groups, own_ref, other_ref, *refs):
    found, out_refs = refs[:groups], refs[groups:]
    rows = found[0].shape[0] // 2

    def pick(step, half):
        columns = slice(step * depth, (step + 1) * depth)
        return jnp.concatenate([f[half * rows : (half + 1) * rows, columns] for f in found], 0)

    for steps, out_ref in zip(jobs, out_refs):
        total = None
        for half, ref in enumerate((own_ref, other_ref)):
            grads = jnp.concatenate([pick(step, half) for step in steps], 1)
            term = dot(ref[...], grads, 0, 0)
            total = term if total is None else total + term
        out_ref[...] = total.astype(out_ref.dtype)


def products(pair, found, depth, jobs, dtypes):
    groups = len(found)
    tokens, wide = pair[0].shape
    count = sum(len(steps) for steps in jobs)
    return pl.pallas_call(
        functools.partial(product_kernel, jobs, depth, groups),
        out_shape=[
            jax.ShapeDtypeStruct((wide, len(steps) * depth), dtype)
            for steps, dtype in zip(jobs, dtypes)
        ],
        compiler_params=SMALL,
        cost_estimate=cost(4 * tokens * wide * count * depth, 4 * tokens * wide),
        name="products",
    )(*pair, *found)


def kv_kernel(rows, mine_ref, arrived_ref, mask_ref, *out_refs):
    place = lax.axis_index("tensor")
    chip, core = place // 2, place % 2
    for step, out_ref in enumerate(out_refs):
        for half in range(2):
            start = ((chip ^ step) * 2 + (core ^ half)) * rows
            span = pl.ds(pl.multiple_of(start, rows), rows)
            total = mine_ref[span, :] + arrived_ref[span, :].astype(F32)
            keep = mask_ref[span, :].astype(F32)
            out_ref[half * rows : (half + 1) * rows, :] = (total * keep).astype(BF16)


def kv_blocks(mine, arrived, mask, rows):
    length, depth = mine.shape
    count = length // (2 * rows)
    return pl.pallas_call(
        functools.partial(kv_kernel, rows),
        out_shape=[jax.ShapeDtypeStruct((2 * rows, depth), BF16)] * count,
        compiler_params=SMALL,
        cost_estimate=cost(0, 2 * mine.nbytes),
        name="kv_blocks",
    )(mine, arrived, mask)


def per_device(inputs, queries, keys_values, out_grad, weight_mask, clip_mask):
    depth = keys_values.shape[1]
    rows = inputs.shape[0]
    groups = lax.axis_size("dp")
    chips = lax.axis_size("tensor") // 2
    block = weight_mask.shape[0]

    other = swap(keys_values, "tensor", 1)
    parts = send_rows(inputs, block)

    query_grad, mine, theirs = attention(keys_values, other, queries, out_grad)
    mine, parts = lax.optimization_barrier((mine, parts))
    arrived = swap(theirs, "tensor", 1)
    blocks = kv_blocks(mine, arrived, clip_mask, rows)

    blocks = [b if s == 0 else swap(b, "tensor", 2 * s) for s, b in enumerate(blocks)]
    parts, places = pass_rows(parts, block)
    blocks, parts = lax.optimization_barrier((blocks, parts))
    order = sorted(range(chips), key=lambda s: [(s >> b) & 1 for b in range(8)])
    evens, odds = order[: chips // 2], order[chips // 2 :]

    wide = block // 2
    outputs = []
    for cut in range(2):
        columns, entries, first = slice(cut * wide, (cut + 1) * wide), [], 0
        for source in places:
            for array, span in source:
                entries.append((array, span, columns, first))
                first += span.stop - span.start
        outputs.append(((groups * rows, wide), entries))
    near, far = [(own, swap(own, "tensor", 1)) for own in lay(parts, outputs)]

    stacked = jnp.concatenate(blocks, 1)
    found = [stacked if s == 0 else swap(stacked, "dp", s) for s in range(groups)]

    def send(value, step):
        return swap(value.astype(BF16), "tensor", 2 * step)

    away = list(range(2, chips))
    straight = products(far, found, depth, [(s,) for s in away], [BF16] * len(away))
    straight, found = lax.optimization_barrier((straight, found))
    straight = [send(value, s) for value, s in zip(straight, away)]
    (first,) = products(near, found, depth, [tuple(odds)], [BF16])
    sent = send(first, 1)
    (even,) = products(near, found, depth, [tuple(evens)], [F32])
    own, nearest = products(far, found, depth, [(0,), (1,)], [F32, BF16])
    sent, straight = lax.optimization_barrier((sent, straight))
    terms = [even, sent]
    columns, bit = chips // 2 * depth, 1
    while columns > depth:
        columns, bit = columns // 2, bit * 2
        away = sum(t[:, columns : 2 * columns].astype(F32) for t in terms).astype(BF16)
        terms.append(send(away, bit))
    nearest, _ = lax.optimization_barrier((nearest, away))
    straight.append(send(nearest, 1))
    upper = sum(t[:, :depth].astype(F32) for t in terms)
    lower = own + sum(t.astype(F32) for t in straight)
    summed = jnp.concatenate([upper, lower], 0)
    weight_grad = jnp.where(weight_mask == 1, summed, 0.0)
    return (query_grad, weight_grad)


def solution(mesh):
    spec = P("dp", "tensor")
    in_specs = (P(("dp", "tensor"), None), spec, spec, spec, spec, spec)
    return jax.shard_map(
        per_device, mesh=mesh, in_specs=in_specs, out_specs=(spec, spec), check_vma=False
    )
```

```python
import functools
import math

import jax
import jax.numpy as jnp
from jax import lax
from jax.experimental import pallas as pl
from jax.experimental.pallas import tpu as pltpu
from jax.sharding import PartitionSpec as P

F32 = jnp.float32
BF16 = jnp.bfloat16
VMEM_LIMIT = 50 * 2**20
SHARE = 4
IN_ORDER = pltpu.CompilerParams(
    vmem_limit_bytes=VMEM_LIMIT, dimension_semantics=("arbitrary",)
)


SMALL = pltpu.CompilerParams(vmem_limit_bytes=16 * 2**20)


def cost(flops, moved, exponents=0):
    return pl.CostEstimate(flops=flops, bytes_accessed=moved, transcendentals=exponents)


TINY = cost(0, 2**16)


def swap(value, axis, mask):
    pairs = [(source, source ^ mask) for source in range(lax.axis_size(axis))]
    return lax.ppermute(value, axis, pairs)


def dot(left, right, left_dim, right_dim):
    dims = (((left_dim,), (right_dim,)), ((), ()))
    return lax.dot_general(left, right, dims, preferred_element_type=F32)


def attention_kernel(height, own_ref, other_ref, q_ref, up_ref, dq_ref, mine_ref, theirs_ref, k_ref, v_ref, dk_ref, dv_ref):
    length, depth = q_ref.shape
    factor = depth**-0.5
    power = factor * math.log2(math.e)
    head = pl.program_id(0)
    is_even = lax.axis_index("tensor") % 2 == 0

    @pl.when(head == 0)
    def _():
        k_ref[...] = jnp.where(is_even, own_ref[...], other_ref[...])
        v_ref[...] = jnp.where(is_even, other_ref[...], own_ref[...])
        dk_ref[...] = jnp.zeros_like(dk_ref)
        dv_ref[...] = jnp.zeros_like(dv_ref)

    half = height // 2
    key_place = lax.broadcasted_iota(jnp.int32, (half, half), 0)
    query_place = lax.broadcasted_iota(jnp.int32, (half, half), 1)
    visible = key_place <= query_place

    def merge(reduce, join, long, short):
        long = reduce(long, axis=0, keepdims=True)
        short = reduce(short, axis=0, keepdims=True)
        return jnp.concatenate([long[:, :half], join(long[:, half:], short)], 1)

    for block in reversed(range(length // height)):
        first = block * height
        middle = first + half
        finish = first + height
        query, upstream = q_ref[first:finish], up_ref[first:finish]
        query_end, upstream_end = query[half:], upstream[half:]
        keys, values = k_ref[:middle], v_ref[:middle]
        keys_end, values_end = k_ref[middle:finish], v_ref[middle:finish]
        scores = dot(keys, query, 1, 1)
        scores_end = dot(keys_end, query_end, 1, 1)
        product = dot(values, upstream, 1, 1)
        product_end = dot(values_end, upstream_end, 1, 1)
        corner = jnp.where(visible, scores[first:, :half], -jnp.inf)
        corner = jnp.concatenate([corner, scores[first:, half:]], 1)
        scores = corner if block == 0 else jnp.concatenate([scores[:first], corner], 0)
        scores_end = jnp.where(visible, scores_end, -jnp.inf)
        biggest = merge(jnp.max, jnp.maximum, scores, scores_end)
        weights = jnp.exp2((scores - biggest) * power)
        weights_end = jnp.exp2((scores_end - biggest[:, half:]) * power)
        scale = 1.0 / merge(jnp.sum, jnp.add, weights, weights_end)
        center = merge(jnp.sum, jnp.add, weights * product, weights_end * product_end) * scale
        weights = weights * scale
        weights_end = weights_end * scale[:, half:]
        grad = (weights * (product - center) * factor).astype(BF16)
        grad_end = (weights_end * (product_end - center[:, half:]) * factor).astype(BF16)
        dv_ref[:middle] += dot(weights.astype(BF16), upstream, 1, 0)
        dv_ref[middle:finish] += dot(weights_end.astype(BF16), upstream_end, 1, 0)
        dk_ref[:middle] += dot(grad, query, 1, 0)
        dk_ref[middle:finish] += dot(grad_end, query_end, 1, 0)
        query_grad = dot(grad, keys, 0, 0)
        dq_ref[first:middle] = query_grad[:half].astype(BF16)
        dq_ref[middle:finish] = (query_grad[half:] + dot(grad_end, keys_end, 0, 0)).astype(BF16)

    @pl.when(head == pl.num_programs(0) - 1)
    def _():
        mine_ref[...] = jnp.where(is_even, dk_ref[...], dv_ref[...])
        theirs_ref[...] = jnp.where(is_even, dv_ref[...], dk_ref[...])


def attention(own, other, queries, out_grad):
    length, width = queries.shape
    depth = own.shape[1]
    height = min(512, length)
    column = pl.BlockSpec((length, depth), lambda h: (0, h))
    whole = pl.BlockSpec((length, depth), lambda h: (0, 0))
    sums = jax.ShapeDtypeStruct((length, depth), F32)
    return pl.pallas_call(
        functools.partial(attention_kernel, height),
        grid=(width // depth,),
        in_specs=[whole, whole, column, column],
        out_specs=[column, whole, whole],
        out_shape=[jax.ShapeDtypeStruct((length, width), BF16), sums, sums],
        scratch_shapes=[
            pltpu.VMEM((length, depth), BF16),
            pltpu.VMEM((length, depth), BF16),
            pltpu.VMEM((length, depth), F32),
            pltpu.VMEM((length, depth), F32),
        ],
        compiler_params=IN_ORDER,
        cost_estimate=cost(
            20 * length * length * width,
            6 * queries.nbytes,
            length * length * width // depth,
        ),
        name="attention",
    )(own, other, queries, out_grad)


def spread_kernel(plan, stride, source_ref, *out_refs):
    wide = out_refs[0].shape[1]
    place = lax.axis_index("dp")
    for out, first, step, low, high in plan:
        start = pl.multiple_of((place ^ step) * stride, 128)
        out_refs[out][first : first + high - low] = source_ref[low:high, pl.ds(start, wide)]


def spread(source, stride, wide, plan):
    heights = {}
    for out, first, _, low, high in plan:
        heights[out] = max(heights.get(out, 0), first + high - low)
    return pl.pallas_call(
        functools.partial(spread_kernel, plan, stride),
        out_shape=[
            jax.ShapeDtypeStruct((heights[out], wide), source.dtype) for out in sorted(heights)
        ],
        compiler_params=SMALL,
        cost_estimate=TINY,
        name="spread",
    )(source)


def lay(sources, outputs):
    def kernel(*refs):
        for out_ref, (_, entries) in zip(refs[len(sources) :], outputs):
            for source, rows, columns, first in entries:
                height = rows.stop - rows.start
                out_ref[first : first + height] = refs[source][rows, columns]

    return pl.pallas_call(
        kernel,
        out_shape=[jax.ShapeDtypeStruct(shape, sources[0].dtype) for shape, _ in outputs],
        compiler_params=SMALL,
        cost_estimate=TINY,
        name="lay",
    )(*sources)


def send_rows(inputs, stride, wide):
    rows = inputs.shape[0]
    groups = lax.axis_size("dp")
    if groups != 4:
        parts = spread(inputs, stride, wide, [(s, 0, s, 0, rows) for s in range(groups)])
        return [part if s == 0 else swap(part, "dp", s) for s, part in enumerate(parts)]
    half = rows // 2
    own, left, right = spread(
        inputs,
        stride,
        wide,
        [(0, 0, 0, 0, rows), (1, 0, 1, 0, rows), (1, rows, 3, 0, half), (2, 0, 2, 0, rows),
         (2, rows, 3, half, rows)],
    )
    return [own, swap(left, "dp", 1), swap(right, "dp", 2)]


def pass_rows(parts, wide):
    rows = parts[0].shape[0]
    groups = lax.axis_size("dp")
    if groups != 4:
        return parts, [[(s, slice(0, rows))] for s in range(groups)]
    own, left, right = parts
    half = rows // 2
    tail = slice(rows, rows + half)
    every = slice(None)
    upper, lower = lay(
        [left, right],
        [((half, wide), [(0, tail, every, 0)]), ((half, wide), [(1, tail, every, 0)])],
    )
    upper, lower = swap(upper, "dp", 2), swap(lower, "dp", 1)
    whole, part = slice(0, rows), slice(0, half)
    places = [[(0, whole)], [(1, whole)], [(2, whole)], [(3, part), (4, part)]]
    return [own, left, right, upper, lower], places


def product_kernel(jobs, depth, groups, own_ref, other_ref, *refs):
    found, out_refs = refs[:groups], refs[groups:]
    rows = found[0].shape[0] // 2

    def pick(step, half):
        columns = slice(step * depth, (step + 1) * depth)
        return jnp.concatenate([f[half * rows : (half + 1) * rows, columns] for f in found], 0)

    for (steps, low, high, _), out_ref in zip(jobs, out_refs):
        total = None
        for half, ref in enumerate((own_ref, other_ref)):
            grads = jnp.concatenate([pick(step, half) for step in steps], 1)
            term = dot(ref[:, low:high], grads, 0, 0)
            total = term if total is None else total + term
        out_ref[...] = total.astype(out_ref.dtype)


def products(pair, found, depth, jobs):
    tokens = pair[0].shape[0]
    count = sum(len(steps) * (high - low) for steps, low, high, _ in jobs)
    return pl.pallas_call(
        functools.partial(product_kernel, jobs, depth, len(found)),
        out_shape=[
            jax.ShapeDtypeStruct((high - low, len(steps) * depth), dtype)
            for steps, low, high, dtype in jobs
        ],
        compiler_params=SMALL,
        cost_estimate=cost(4 * tokens * count * depth, 2**20),
        name="products",
    )(*pair, *found)


def kv_kernel(rows, mine_ref, arrived_ref, mask_ref, whole_ref, *out_refs):
    place = lax.axis_index("tensor")
    chip, core = place // 2, place % 2
    keep = mask_ref[...].astype(F32)
    whole_ref[...] = ((mine_ref[...] + arrived_ref[...]) * keep).astype(BF16)
    for step, out_ref in enumerate(out_refs):
        for half in range(2):
            start = ((chip ^ step) * 2 + (core ^ half)) * rows
            span = pl.ds(pl.multiple_of(start, rows), rows)
            out_ref[half * rows : (half + 1) * rows, :] = whole_ref[span, :]


def kv_blocks(mine, arrived, mask, rows):
    length, depth = mine.shape
    count = length // (2 * rows)
    return pl.pallas_call(
        functools.partial(kv_kernel, rows),
        out_shape=[jax.ShapeDtypeStruct((length, depth), BF16)]
        + [jax.ShapeDtypeStruct((2 * rows, depth), BF16)] * count,
        compiler_params=SMALL,
        cost_estimate=TINY,
        name="kv_blocks",
    )(mine, arrived, mask)


def own_kernel(wide, rows_ref, grads_ref, *out_refs):
    place = lax.axis_index("dp")
    for step, out_ref in enumerate(out_refs):
        start = pl.multiple_of((place ^ step) * wide, wide)
        part = rows_ref[:, pl.ds(start, wide)]
        out_ref[...] = dot(part, grads_ref[...], 0, 0).astype(out_ref.dtype)


def own_products(gathered, grads, groups):
    wide = gathered.shape[1] // groups
    depth = grads.shape[1]
    return pl.pallas_call(
        functools.partial(own_kernel, wide),
        out_shape=[
            jax.ShapeDtypeStruct((wide, depth), BF16 if step else F32) for step in range(groups)
        ],
        compiler_params=pltpu.CompilerParams(vmem_limit_bytes=32 * 2**20),
        cost_estimate=cost(2 * math.prod(gathered.shape) * depth, gathered.nbytes),
        name="own_products",
    )(gathered, grads)


def per_device(inputs, queries, keys_values, out_grad, weight_mask, clip_mask):
    depth = keys_values.shape[1]
    rows = inputs.shape[0]
    groups = lax.axis_size("dp")
    chips = lax.axis_size("tensor") // 2
    block = weight_mask.shape[0]

    extra = block // SHARE // 128 * 128
    wide = (block - extra) // 2
    tails = [inputs[:, g * block + 2 * wide : (g + 1) * block] for g in range(groups)]
    gathered = lax.all_gather(jnp.concatenate(tails, 1), "tensor", axis=0, tiled=True)

    other = swap(keys_values, "tensor", 1)
    parts = send_rows(inputs, block, 2 * wide)

    query_grad, mine, theirs = attention(keys_values, other, queries, out_grad)
    mine, parts = lax.optimization_barrier((mine, parts))
    arrived = swap(theirs, "tensor", 1)
    grads, *blocks = kv_blocks(mine, arrived, clip_mask, rows)

    blocks = [b if s == 0 else swap(b, "tensor", 2 * s) for s, b in enumerate(blocks)]
    parts, places = pass_rows(parts, 2 * wide)
    blocks, parts = lax.optimization_barrier((blocks, parts))
    order = sorted(range(chips), key=lambda s: [(s >> b) & 1 for b in range(8)])
    evens, odds = order[: chips // 2], order[chips // 2 :]
    stacked = jnp.concatenate(blocks, 1)
    found = [stacked if s == 0 else swap(stacked, "dp", s) for s in range(groups)]

    entries, first = [], 0
    for source in places:
        for array, span in source:
            entries.append((array, span, slice(None), first))
            first += span.stop - span.start
    (packed,) = lay(parts, [((first, 2 * wide), entries)])
    pair = (packed, swap(packed, "tensor", 1))

    def send(value, step):
        return swap(value.astype(BF16), "tensor", 2 * step)

    far, near = (wide, 2 * wide), (0, wide)
    away = list(range(2, chips))
    straight = products(pair, found, depth, [((s,), *far, BF16) for s in away])
    straight, found = lax.optimization_barrier((straight, found))
    straight = [send(value, s) for value, s in zip(straight, away)]
    (first,) = products(pair, found, depth, [(tuple(odds), *near, BF16)])
    sent = send(first, 1)
    found, grads, _ = lax.optimization_barrier((found, grads, first))
    even, own, nearest = products(
        pair, found, depth, [(tuple(evens), *near, F32), ((0,), *far, F32), ((1,), *far, BF16)]
    )
    ends = own_products(gathered, grads, groups)
    ends = [e if s == 0 else swap(e, "dp", s) for s, e in enumerate(ends)]
    sent, straight, ends = lax.optimization_barrier((sent, straight, ends))
    terms = [even, sent]
    columns, bit = chips // 2 * depth, 1
    while columns > depth:
        columns, bit = columns // 2, bit * 2
        away = sum(t[:, columns : 2 * columns].astype(F32) for t in terms).astype(BF16)
        terms.append(send(away, bit))
    nearest, _ = lax.optimization_barrier((nearest, away))
    straight.append(send(nearest, 1))
    upper = sum(t[:, :depth].astype(F32) for t in terms)
    lower = own + sum(t.astype(F32) for t in straight)
    last = sum(e.astype(F32) for e in ends)
    summed = jnp.concatenate([upper, lower, last], 0)
    weight_grad = jnp.where(weight_mask == 1, summed, 0.0)
    return (query_grad, weight_grad)


def solution(mesh):
    spec = P("dp", "tensor")
    in_specs = (P(("dp", "tensor"), None), spec, spec, spec, spec, spec)
    return jax.shard_map(
        per_device, mesh=mesh, in_specs=in_specs, out_specs=(spec, spec), check_vma=False
    )
```

```python
import functools
import math

import jax
import jax.numpy as jnp
from jax import lax
from jax.experimental import pallas as pl
from jax.experimental.pallas import tpu as pltpu
from jax.sharding import PartitionSpec as P

F32 = jnp.float32
BF16 = jnp.bfloat16
VMEM_LIMIT = 50 * 2**20
IN_ORDER = pltpu.CompilerParams(
    vmem_limit_bytes=VMEM_LIMIT, dimension_semantics=("arbitrary",)
)


SMALL = pltpu.CompilerParams(vmem_limit_bytes=16 * 2**20)


def cost(flops, moved, exponents=0):
    return pl.CostEstimate(flops=flops, bytes_accessed=moved, transcendentals=exponents)


TINY = cost(0, 2**10)


def swap(value, axis, mask):
    pairs = [(source, source ^ mask) for source in range(lax.axis_size(axis))]
    return lax.ppermute(value, axis, pairs)


def dot(left, right, left_dim, right_dim):
    dims = (((left_dim,), (right_dim,)), ((), ()))
    return lax.dot_general(left, right, dims, preferred_element_type=F32)


def attention_kernel(height, own_ref, other_ref, q_ref, up_ref, dq_ref, mine_ref, theirs_ref, k_ref, v_ref, dk_ref, dv_ref):
    length, depth = q_ref.shape
    factor = depth**-0.5
    power = factor * math.log2(math.e)
    head = pl.program_id(0)
    is_even = lax.axis_index("tensor") % 2 == 0

    @pl.when(head == 0)
    def _():
        k_ref[...] = jnp.where(is_even, own_ref[...], other_ref[...])
        v_ref[...] = jnp.where(is_even, other_ref[...], own_ref[...])
        dk_ref[...] = jnp.zeros_like(dk_ref)
        dv_ref[...] = jnp.zeros_like(dv_ref)

    half = height // 2
    key_place = lax.broadcasted_iota(jnp.int32, (half, half), 0)
    query_place = lax.broadcasted_iota(jnp.int32, (half, half), 1)
    visible = key_place <= query_place

    def merge(reduce, join, long, short):
        long = reduce(long, axis=0, keepdims=True)
        short = reduce(short, axis=0, keepdims=True)
        return jnp.concatenate([long[:, :half], join(long[:, half:], short)], 1)

    for block in reversed(range(length // height)):
        first = block * height
        middle = first + half
        finish = first + height
        query, upstream = q_ref[first:finish], up_ref[first:finish]
        query_end, upstream_end = query[half:], upstream[half:]
        keys, values = k_ref[:middle], v_ref[:middle]
        keys_end, values_end = k_ref[middle:finish], v_ref[middle:finish]
        scores = dot(keys, query, 1, 1)
        scores_end = dot(keys_end, query_end, 1, 1)
        product = dot(values, upstream, 1, 1)
        product_end = dot(values_end, upstream_end, 1, 1)
        corner = jnp.where(visible, scores[first:, :half], -jnp.inf)
        corner = jnp.concatenate([corner, scores[first:, half:]], 1)
        scores = corner if block == 0 else jnp.concatenate([scores[:first], corner], 0)
        scores_end = jnp.where(visible, scores_end, -jnp.inf)
        biggest = merge(jnp.max, jnp.maximum, scores, scores_end)
        weights = jnp.exp2((scores - biggest) * power)
        weights_end = jnp.exp2((scores_end - biggest[:, half:]) * power)
        scale = 1.0 / merge(jnp.sum, jnp.add, weights, weights_end)
        center = merge(jnp.sum, jnp.add, weights * product, weights_end * product_end) * scale
        weights = weights * scale
        weights_end = weights_end * scale[:, half:]
        grad = (weights * (product - center) * factor).astype(BF16)
        grad_end = (weights_end * (product_end - center[:, half:]) * factor).astype(BF16)
        dv_ref[:middle] += dot(weights.astype(BF16), upstream, 1, 0)
        dv_ref[middle:finish] += dot(weights_end.astype(BF16), upstream_end, 1, 0)
        dk_ref[:middle] += dot(grad, query, 1, 0)
        dk_ref[middle:finish] += dot(grad_end, query_end, 1, 0)
        query_grad = dot(grad, keys, 0, 0)
        dq_ref[first:middle] = query_grad[:half].astype(BF16)
        dq_ref[middle:finish] = (query_grad[half:] + dot(grad_end, keys_end, 0, 0)).astype(BF16)

    @pl.when(head == pl.num_programs(0) - 1)
    def _():
        mine_ref[...] = jnp.where(is_even, dk_ref[...], dv_ref[...])
        theirs_ref[...] = jnp.where(is_even, dv_ref[...], dk_ref[...])


def attention(own, other, queries, out_grad):
    length, width = queries.shape
    depth = own.shape[1]
    height = min(512, length)
    column = pl.BlockSpec((length, depth), lambda h: (0, h))
    whole = pl.BlockSpec((length, depth), lambda h: (0, 0))
    sums = jax.ShapeDtypeStruct((length, depth), F32)
    return pl.pallas_call(
        functools.partial(attention_kernel, height),
        grid=(width // depth,),
        in_specs=[whole, whole, column, column],
        out_specs=[column, whole, whole],
        out_shape=[jax.ShapeDtypeStruct((length, width), BF16), sums, sums],
        scratch_shapes=[
            pltpu.VMEM((length, depth), BF16),
            pltpu.VMEM((length, depth), BF16),
            pltpu.VMEM((length, depth), F32),
            pltpu.VMEM((length, depth), F32),
        ],
        compiler_params=IN_ORDER,
        cost_estimate=cost(
            20 * length * length * width,
            6 * queries.nbytes,
            length * length * width // depth,
        ),
        name="attention",
    )(own, other, queries, out_grad)


def spread_kernel(plan, source_ref, *out_refs):
    wide = out_refs[0].shape[1]
    place = lax.axis_index("dp")
    for out, first, step, low, high in plan:
        start = pl.multiple_of((place ^ step) * wide, wide)
        out_refs[out][first : first + high - low] = source_ref[low:high, pl.ds(start, wide)]


def spread(source, wide, plan):
    heights = {}
    for out, first, _, low, high in plan:
        heights[out] = max(heights.get(out, 0), first + high - low)
    return pl.pallas_call(
        functools.partial(spread_kernel, plan),
        out_shape=[
            jax.ShapeDtypeStruct((heights[out], wide), source.dtype) for out in sorted(heights)
        ],
        compiler_params=SMALL,
        cost_estimate=TINY,
        name="spread",
    )(source)


def lay(sources, outputs):
    def kernel(*refs):
        for out_ref, (_, entries) in zip(refs[len(sources) :], outputs):
            for source, rows, columns, first in entries:
                height = rows.stop - rows.start
                out_ref[first : first + height] = refs[source][rows, columns]

    return pl.pallas_call(
        kernel,
        out_shape=[jax.ShapeDtypeStruct(shape, sources[0].dtype) for shape, _ in outputs],
        compiler_params=SMALL,
        cost_estimate=TINY,
        name="lay",
    )(*sources)


def send_rows(inputs, wide):
    rows = inputs.shape[0]
    groups = lax.axis_size("dp")
    if groups != 4:
        parts = spread(inputs, wide, [(s, 0, s, 0, rows) for s in range(groups)])
        return [part if s == 0 else swap(part, "dp", s) for s, part in enumerate(parts)]
    half = rows // 2
    own, left, right = spread(
        inputs,
        wide,
        [(0, 0, 0, 0, rows), (1, 0, 1, 0, rows), (1, rows, 3, 0, half), (2, 0, 2, 0, rows),
         (2, rows, 3, half, rows)],
    )
    return [own, swap(left, "dp", 1), swap(right, "dp", 2)]


def pass_rows(parts, wide):
    rows = parts[0].shape[0]
    groups = lax.axis_size("dp")
    if groups != 4:
        return parts, [[(s, slice(0, rows))] for s in range(groups)]
    own, left, right = parts
    half = rows // 2
    tail = slice(rows, rows + half)
    every = slice(None)
    upper, lower = lay(
        [left, right],
        [((half, wide), [(0, tail, every, 0)]), ((half, wide), [(1, tail, every, 0)])],
    )
    upper, lower = swap(upper, "dp", 2), swap(lower, "dp", 1)
    whole, part = slice(0, rows), slice(0, half)
    places = [[(0, whole)], [(1, whole)], [(2, whole)], [(3, part), (4, part)]]
    return [own, left, right, upper, lower], places


def product_kernel(jobs, depth, held, groups, own_ref, other_ref, *refs):
    count = len(held) * groups
    found, out_refs = refs[:count], refs[count:]
    rows = found[0].shape[0] // 2

    def pick(step, half):
        for index, steps in enumerate(held):
            if step in steps:
                place = steps.index(step) * depth
                part = found[index * groups : (index + 1) * groups]
        span = slice(half * rows, (half + 1) * rows)
        return jnp.concatenate([f[span, place : place + depth] for f in part], 0)

    for (steps, low, high, _), out_ref in zip(jobs, out_refs):
        total = None
        for half, ref in enumerate((own_ref, other_ref)):
            grads = jnp.concatenate([pick(step, half) for step in steps], 1)
            term = dot(ref[:, low:high], grads, 0, 0)
            total = term if total is None else total + term
        out_ref[...] = total.astype(out_ref.dtype)


def products(pair, depth, found, jobs):
    held = [steps for steps, _ in found]
    groups = len(found[0][1])
    return pl.pallas_call(
        functools.partial(product_kernel, jobs, depth, held, groups),
        out_shape=[
            jax.ShapeDtypeStruct((high - low, len(steps) * depth), dtype)
            for steps, low, high, dtype in jobs
        ],
        compiler_params=SMALL,
        cost_estimate=TINY,
        name="products",
    )(*pair, *[array for _, arrays in found for array in arrays])


def kv_kernel(rows, mine_ref, arrived_ref, mask_ref, *out_refs):
    place = lax.axis_index("tensor")
    chip, core = place // 2, place % 2
    for step, out_ref in enumerate(out_refs):
        for half in range(2):
            start = ((chip ^ step) * 2 + (core ^ half)) * rows
            span = pl.ds(pl.multiple_of(start, rows), rows)
            total = mine_ref[span, :] + arrived_ref[span, :]
            keep = mask_ref[span, :].astype(F32)
            out_ref[half * rows : (half + 1) * rows, :] = (total * keep).astype(BF16)


def kv_blocks(mine, arrived, mask, rows):
    length, depth = mine.shape
    count = length // (2 * rows)
    return pl.pallas_call(
        functools.partial(kv_kernel, rows),
        out_shape=[jax.ShapeDtypeStruct((2 * rows, depth), BF16)] * count,
        compiler_params=SMALL,
        cost_estimate=TINY,
        name="kv_blocks",
    )(mine, arrived, mask)


def per_device(inputs, queries, keys_values, out_grad, weight_mask, clip_mask):
    depth = keys_values.shape[1]
    rows = inputs.shape[0]
    groups = lax.axis_size("dp")
    chips = lax.axis_size("tensor") // 2
    block = weight_mask.shape[0]

    wide = block // 2
    other = swap(keys_values, "tensor", 1)
    parts = send_rows(inputs, block)

    query_grad, mine, theirs = attention(keys_values, other, queries, out_grad)
    mine, parts = lax.optimization_barrier((mine, parts))
    arrived = swap(theirs, "tensor", 1)
    blocks = kv_blocks(mine, arrived, clip_mask, rows)

    blocks = [b if s == 0 else swap(b, "tensor", 2 * s) for s, b in enumerate(blocks)]
    parts, places = pass_rows(parts, block)
    blocks, parts = lax.optimization_barrier((blocks, parts))
    order = sorted(range(chips), key=lambda s: [(s >> b) & 1 for b in range(8)])
    evens, odds = order[: chips // 2], order[chips // 2 :]

    def gather(steps, values):
        stacked = jnp.concatenate(values, 1)
        return steps, [stacked if s == 0 else swap(stacked, "dp", s) for s in range(groups)]

    entries, first = [], 0
    for source in places:
        for array, span in source:
            entries.append((array, span, slice(None), first))
            first += span.stop - span.start
    (packed,) = lay(parts, [((first, 2 * wide), entries)])
    pair = (packed, swap(packed, "tensor", 1))

    def send(value, step):
        return swap(value.astype(BF16), "tensor", 2 * step)

    far, near = (wide, 2 * wide), (0, wide)
    away, close = list(range(2, chips)), [0, 1]
    far_found = gather(away, [blocks[s] for s in away])
    straight = products(pair, depth, [far_found], [((s,), *far, BF16) for s in away])
    values, straight = lax.optimization_barrier(([blocks[s] for s in close], straight))
    arrived = []
    for value, step in zip(straight, away):
        if arrived:
            value, arrived[-1] = lax.optimization_barrier((value, arrived[-1]))
        arrived.append(send(value, step))
    found = [far_found, gather(close, values)]
    (first,) = products(pair, depth, found, [(tuple(odds), *near, BF16)])
    sent = send(first, 1)
    arrays, _ = lax.optimization_barrier(([arrays for _, arrays in found], first))
    found = [(away, arrays[0]), (close, arrays[1])]
    even, own, nearest = products(
        pair, depth, found, [(tuple(evens), *near, F32), ((0,), *far, F32), ((1,), *far, BF16)]
    )
    terms = [even, sent]
    columns, bit = chips // 2 * depth, 1
    while columns > depth:
        columns, bit = columns // 2, bit * 2
        away = sum(t[:, columns : 2 * columns].astype(F32) for t in terms).astype(BF16)
        terms.append(send(away, bit))
    nearest, arrived[-1] = lax.optimization_barrier((nearest, arrived[-1]))
    arrived.append(send(nearest, 1))
    upper = sum(t[:, :depth].astype(F32) for t in terms)
    lower = own + sum(t.astype(F32) for t in arrived)
    summed = jnp.concatenate([upper, lower], 0)
    weight_grad = jnp.where(weight_mask == 1, summed, 0.0)
    return (query_grad, weight_grad)


def solution(mesh):
    spec = P("dp", "tensor")
    in_specs = (P(("dp", "tensor"), None), spec, spec, spec, spec, spec)
    return jax.shard_map(
        per_device, mesh=mesh, in_specs=in_specs, out_specs=(spec, spec), check_vma=False
    )
```

```python
import functools
import math

import jax
import jax.numpy as jnp
from jax import lax
from jax.experimental import pallas as pl
from jax.experimental.pallas import tpu as pltpu
from jax.sharding import PartitionSpec as P

F32 = jnp.float32
BF16 = jnp.bfloat16
VMEM_LIMIT = 40 * 2**20
IN_ORDER = pltpu.CompilerParams(
    vmem_limit_bytes=VMEM_LIMIT, dimension_semantics=("arbitrary",)
)


SMALL = pltpu.CompilerParams(vmem_limit_bytes=16 * 2**20)


def cost(flops, moved, exponents=0):
    return pl.CostEstimate(flops=flops, bytes_accessed=moved, transcendentals=exponents)


TINY, LONG = cost(0, 2**10), cost(2 * 10**10, 2**20)


def swap(value, axis, mask):
    pairs = [(source, source ^ mask) for source in range(lax.axis_size(axis))]
    return lax.ppermute(value, axis, pairs)


def dot(left, right, left_dim, right_dim):
    dims = (((left_dim,), (right_dim,)), ((), ()))
    return lax.dot_general(left, right, dims, preferred_element_type=F32)


def attention_kernel(
    height, heads, own_ref, other_ref, q_ref, up_ref, dq_ref, mine_ref, theirs_ref,
    k_ref, v_ref, dk_ref, dv_ref,
):
    length, depth = k_ref.shape
    factor = depth**-0.5
    power = factor * math.log2(math.e)
    step = pl.program_id(0)
    is_even = lax.axis_index("tensor") % 2 == 0

    @pl.when(step == 0)
    def _():
        k_ref[...] = jnp.where(is_even, own_ref[...], other_ref[...])
        v_ref[...] = jnp.where(is_even, other_ref[...], own_ref[...])
        dk_ref[...] = jnp.zeros_like(dk_ref)
        dv_ref[...] = jnp.zeros_like(dv_ref)

    half = height // 2
    key_place = lax.broadcasted_iota(jnp.int32, (half, half), 0)
    query_place = lax.broadcasted_iota(jnp.int32, (half, half), 1)
    visible = key_place <= query_place

    def merge(reduce, join, long, short):
        long = reduce(long, axis=0, keepdims=True)
        short = reduce(short, axis=0, keepdims=True)
        return jnp.concatenate([long[:, :half], join(long[:, half:], short)], 1)

    def load(unit):
        head, block = unit
        span = slice(block * height, (block + 1) * height)
        columns = slice(head * depth, (head + 1) * depth)
        middle = block * height + half
        rows, end = slice(0, middle), slice(middle, middle + half)
        return q_ref[span, columns], up_ref[span, columns], rows, end

    def multiply(unit):
        query, upstream, rows, end = load(unit)
        return (
            dot(k_ref[rows], query, 1, 1),
            dot(k_ref[end], query[half:], 1, 1),
            dot(v_ref[rows], upstream, 1, 1),
            dot(v_ref[end], upstream[half:], 1, 1),
        )

    def normalize(unit, scores, scores_end, product, product_end):
        first = unit[1] * height
        corner = jnp.where(visible, scores[first:, :half], -jnp.inf)
        corner = jnp.concatenate([corner, scores[first:, half:]], 1)
        scores = corner if first == 0 else jnp.concatenate([scores[:first], corner], 0)
        scores_end = jnp.where(visible, scores_end, -jnp.inf)
        biggest = merge(jnp.max, jnp.maximum, scores, scores_end)
        weights = jnp.exp2((scores - biggest) * power)
        weights_end = jnp.exp2((scores_end - biggest[:, half:]) * power)
        scale = 1.0 / merge(jnp.sum, jnp.add, weights, weights_end)
        center = merge(jnp.sum, jnp.add, weights * product, weights_end * product_end) * scale
        weights = weights * scale
        weights_end = weights_end * scale[:, half:]
        grad = (weights * (product - center) * factor).astype(BF16)
        grad_end = (weights_end * (product_end - center[:, half:]) * factor).astype(BF16)
        return weights.astype(BF16), weights_end.astype(BF16), grad, grad_end

    def collect(unit, weights, weights_end, grad, grad_end):
        query, upstream, rows, end = load(unit)
        columns = slice(unit[0] * depth, (unit[0] + 1) * depth)
        dv_ref[rows] += dot(weights, upstream, 1, 0)
        dv_ref[end] += dot(weights_end, upstream[half:], 1, 0)
        dk_ref[rows] += dot(grad, query, 1, 0)
        dk_ref[end] += dot(grad_end, query[half:], 1, 0)
        query_grad = dot(grad, k_ref[rows], 0, 0)
        tail = query_grad[half:] + dot(grad_end, k_ref[end], 0, 0)
        dq_ref[rows.stop - half : rows.stop, columns] = query_grad[:half].astype(BF16)
        dq_ref[end, columns] = tail.astype(BF16)

    units = [(h, b) for h in range(heads) for b in reversed(range(length // height))]
    held, last = multiply(units[0]), None
    for index, unit in enumerate(units):
        ahead = multiply(units[index + 1]) if index + 1 < len(units) else None
        ready = normalize(unit, *held)
        if last is not None:
            collect(*last)
        last, held = (unit, *ready), ahead
    collect(*last)

    @pl.when(step == pl.num_programs(0) - 1)
    def _():
        mine_ref[...] = jnp.where(is_even, dk_ref[...], dv_ref[...])
        theirs_ref[...] = jnp.where(is_even, dv_ref[...], dk_ref[...])


def attention(own, other, queries, out_grad):
    length, width = queries.shape
    depth = own.shape[1]
    height = min(512, length)
    heads = 2 if width // depth % 2 == 0 else 1
    column = pl.BlockSpec((length, heads * depth), lambda h: (0, h))
    whole = pl.BlockSpec((length, depth), lambda h: (0, 0))
    sums = jax.ShapeDtypeStruct((length, depth), F32)
    return pl.pallas_call(
        functools.partial(attention_kernel, height, heads),
        grid=(width // (heads * depth),),
        in_specs=[whole, whole, column, column],
        out_specs=[column, whole, whole],
        out_shape=[jax.ShapeDtypeStruct((length, width), BF16), sums, sums],
        scratch_shapes=[
            pltpu.VMEM((length, depth), BF16),
            pltpu.VMEM((length, depth), BF16),
            pltpu.VMEM((length, depth), F32),
            pltpu.VMEM((length, depth), F32),
        ],
        compiler_params=IN_ORDER,
        cost_estimate=cost(
            20 * length * length * width,
            6 * queries.nbytes,
            length * length * width // depth,
        ),
        name="attention",
    )(own, other, queries, out_grad)


def spread_kernel(plan, source_ref, *out_refs):
    wide = out_refs[0].shape[1]
    place = lax.axis_index("dp")
    for out, first, step, low, high in plan:
        start = pl.multiple_of((place ^ step) * wide, wide)
        out_refs[out][first : first + high - low] = source_ref[low:high, pl.ds(start, wide)]


def spread(source, wide, plan):
    heights = {}
    for out, first, _, low, high in plan:
        heights[out] = max(heights.get(out, 0), first + high - low)
    return pl.pallas_call(
        functools.partial(spread_kernel, plan),
        out_shape=[
            jax.ShapeDtypeStruct((heights[out], wide), source.dtype) for out in sorted(heights)
        ],
        compiler_params=SMALL,
        cost_estimate=TINY,
        name="spread",
    )(source)


def lay(sources, outputs, hint=TINY):
    def kernel(*refs):
        for out_ref, (_, entries) in zip(refs[len(sources) :], outputs):
            for source, rows, columns, first in entries:
                height = rows.stop - rows.start
                out_ref[first : first + height] = refs[source][rows, columns]

    return pl.pallas_call(
        kernel,
        out_shape=[jax.ShapeDtypeStruct(shape, sources[0].dtype) for shape, _ in outputs],
        compiler_params=SMALL,
        cost_estimate=hint,
        name="lay",
    )(*sources)


def send_rows(inputs, wide):
    rows = inputs.shape[0]
    groups = lax.axis_size("dp")
    if groups != 4:
        parts = spread(inputs, wide, [(s, 0, s, 0, rows) for s in range(groups)])
        return [part if s == 0 else swap(part, "dp", s) for s, part in enumerate(parts)]
    half = rows // 2
    own, left, right = spread(
        inputs,
        wide,
        [(0, 0, 0, 0, rows), (1, 0, 1, 0, rows), (1, rows, 3, 0, half), (2, 0, 2, 0, rows),
         (2, rows, 3, half, rows)],
    )
    return [own, swap(left, "dp", 1), swap(right, "dp", 2)]


def pass_rows(parts, wide):
    rows = parts[0].shape[0]
    groups = lax.axis_size("dp")
    if groups != 4:
        return parts, [[(s, slice(0, rows))] for s in range(groups)]
    own, left, right = parts
    half = rows // 2
    tail = slice(rows, rows + half)
    every = slice(None)
    upper, lower = lay(
        [left, right],
        [((half, wide), [(0, tail, every, 0)]), ((half, wide), [(1, tail, every, 0)])],
    )
    upper, lower = swap(upper, "dp", 2), swap(lower, "dp", 1)
    whole, part = slice(0, rows), slice(0, half)
    places = [[(0, whole)], [(1, whole)], [(2, whole)], [(3, part), (4, part)]]
    return [own, left, right, upper, lower], places


def product_kernel(jobs, depth, own_ref, other_ref, own_grads_ref, other_grads_ref, *out_refs):
    pairs = ((own_ref, own_grads_ref), (other_ref, other_grads_ref))
    for (places, low, high, _), out_ref in zip(jobs, out_refs):
        columns = slice(places[0] * depth, (places[-1] + 1) * depth)
        total = sum(dot(ref[:, low:high], grads[:, columns], 0, 0) for ref, grads in pairs)
        out_ref[...] = total.astype(out_ref.dtype)


def products(pair, grads, depth, jobs, hint=TINY):
    return pl.pallas_call(
        functools.partial(product_kernel, jobs, depth),
        out_shape=[
            jax.ShapeDtypeStruct((high - low, len(places) * depth), dtype)
            for places, low, high, dtype in jobs
        ],
        compiler_params=SMALL,
        cost_estimate=hint,
        name="products",
    )(*pair, *grads)


def kv_kernel(rows, mine_ref, arrived_ref, mask_ref, *out_refs):
    place = lax.axis_index("tensor")
    chip, core = place // 2, place % 2
    for step, out_ref in enumerate(out_refs):
        for half in range(2):
            start = ((chip ^ step) * 2 + (core ^ half)) * rows
            span = pl.ds(pl.multiple_of(start, rows), rows)
            total = mine_ref[span, :] + arrived_ref[span, :].astype(F32)
            keep = mask_ref[span, :].astype(F32)
            out_ref[half * rows : (half + 1) * rows, :] = (total * keep).astype(BF16)


def kv_blocks(mine, arrived, mask, rows):
    length, depth = mine.shape
    count = length // (2 * rows)
    return pl.pallas_call(
        functools.partial(kv_kernel, rows),
        out_shape=[jax.ShapeDtypeStruct((2 * rows, depth), BF16)] * count,
        compiler_params=SMALL,
        cost_estimate=TINY,
        name="kv_blocks",
    )(mine, arrived, mask)


def per_device(inputs, queries, keys_values, out_grad, weight_mask, clip_mask):
    depth = keys_values.shape[1]
    rows = inputs.shape[0]
    groups = lax.axis_size("dp")
    chips = lax.axis_size("tensor") // 2
    block = weight_mask.shape[0]

    other = swap(keys_values, "tensor", 1)
    parts = send_rows(inputs, block)

    query_grad, mine, theirs = attention(keys_values, other, queries, out_grad)
    mine, parts = lax.optimization_barrier((mine, parts))
    arrived = swap(theirs, "tensor", 1)
    blocks = kv_blocks(mine, arrived, clip_mask, rows)

    blocks = [b if s == 0 else swap(b, "tensor", 2 * s) for s, b in enumerate(blocks)]
    parts, places = pass_rows(parts, block)
    blocks, parts = lax.optimization_barrier((blocks, parts))
    order = sorted(range(chips), key=lambda s: [(s >> b) & 1 for b in range(8)])
    evens, odds = order[: chips // 2], order[chips // 2 :]
    stacked = jnp.concatenate([blocks[s] for s in order], 1)
    found = [stacked if s == 0 else swap(stacked, "dp", s) for s in range(groups)]
    whole = (groups * rows, chips * depth)
    halves = [
        (whole, [(s, slice(h * rows, (h + 1) * rows), slice(None), s * rows) for s in range(groups)])
        for h in (0, 1)
    ]
    grads = lay(found, halves, LONG)

    entries, first = [], 0
    for source in places:
        for array, span in source:
            entries.append((array, span, slice(None), first))
            first += span.stop - span.start
    (packed,) = lay(parts, [((first, block), entries)])
    pair = (packed, swap(packed, "tensor", 1))

    def send(value, step):
        return swap(value.astype(BF16), "tensor", 2 * step)

    wide, half = block // 2, chips // 2
    far, near = (wide, block), (0, wide)
    away = list(range(2, chips))
    direct = products(pair, grads, depth, [((order.index(s),), *far, BF16) for s in away])
    direct, grads = lax.optimization_barrier((direct, grads))
    (first,) = products(pair, grads, depth, [(range(half, chips), *near, BF16)], LONG)
    direct = [send(value, s) for value, s in zip(direct, away)]
    sent = send(first, 1)
    grads, _ = lax.optimization_barrier((grads, first))
    jobs = [(range(half), *near, F32), ((0,), *far, F32), ((order.index(1),), *far, BF16)]
    even, own, nearest = products(pair, grads, depth, jobs)
    sent, direct = lax.optimization_barrier((sent, direct))
    terms = [even, sent]
    columns, bit = half * depth, 1
    while columns > depth:
        columns, bit = columns // 2, bit * 2
        value = sum(t[:, columns : 2 * columns].astype(F32) for t in terms).astype(BF16)
        terms.append(send(value, bit))
    nearest, _ = lax.optimization_barrier((nearest, value))
    direct.append(send(nearest, 1))
    upper = sum(t[:, :depth].astype(F32) for t in terms)
    lower = own + sum(t.astype(F32) for t in direct)
    summed = jnp.concatenate([upper, lower], 0)
    weight_grad = jnp.where(weight_mask == 1, summed, 0.0)
    return (query_grad, weight_grad)


def solution(mesh):
    spec = P("dp", "tensor")
    in_specs = (P(("dp", "tensor"), None), spec, spec, spec, spec, spec)
    return jax.shard_map(
        per_device, mesh=mesh, in_specs=in_specs, out_specs=(spec, spec), check_vma=False
    )
```

```python
import functools
import math

import jax
import jax.numpy as jnp
from jax import lax
from jax.experimental import pallas as pl
from jax.experimental.pallas import tpu as pltpu
from jax.sharding import PartitionSpec as P

F32 = jnp.float32
BF16 = jnp.bfloat16
VMEM_LIMIT = 30 * 2**20
IN_ORDER = pltpu.CompilerParams(
    vmem_limit_bytes=VMEM_LIMIT, dimension_semantics=("arbitrary",)
)


SMALL = pltpu.CompilerParams(vmem_limit_bytes=16 * 2**20)


def cost(flops, moved, exponents=0):
    return pl.CostEstimate(flops=flops, bytes_accessed=moved, transcendentals=exponents)


TINY, LONG = cost(0, 2**10), cost(2 * 10**10, 2**20)


def swap(value, axis, mask):
    pairs = [(source, source ^ mask) for source in range(lax.axis_size(axis))]
    return lax.ppermute(value, axis, pairs)


def dot(left, right, left_dim, right_dim):
    dims = (((left_dim,), (right_dim,)), ((), ()))
    return lax.dot_general(left, right, dims, preferred_element_type=F32)


def attention_kernel(
    height, heads, own_ref, other_ref, q_ref, up_ref, dq_ref, mine_ref, theirs_ref,
    k_ref, v_ref, dk_ref, dv_ref,
):
    length, depth = k_ref.shape
    factor = depth**-0.5
    power = factor * math.log2(math.e)
    step = pl.program_id(0)
    is_even = lax.axis_index("tensor") % 2 == 0

    @pl.when(step == 0)
    def _():
        k_ref[...] = jnp.where(is_even, own_ref[...], other_ref[...])
        v_ref[...] = jnp.where(is_even, other_ref[...], own_ref[...])
        dk_ref[...] = jnp.zeros_like(dk_ref)
        dv_ref[...] = jnp.zeros_like(dv_ref)

    half = height // 2
    key_place = lax.broadcasted_iota(jnp.int32, (half, half), 0)
    query_place = lax.broadcasted_iota(jnp.int32, (half, half), 1)
    visible = key_place <= query_place

    def merge(reduce, join, long, short):
        long = reduce(long, axis=0, keepdims=True)
        short = reduce(short, axis=0, keepdims=True)
        return jnp.concatenate([long[:, :half], join(long[:, half:], short)], 1)

    def load(unit):
        head, block = unit
        span = slice(block * height, (block + 1) * height)
        columns = slice(head * depth, (head + 1) * depth)
        middle = block * height + half
        rows, end = slice(0, middle), slice(middle, middle + half)
        return q_ref[span, columns], up_ref[span, columns], rows, end

    def multiply(unit):
        query, upstream, rows, end = load(unit)
        return (
            dot(k_ref[rows], query, 1, 1),
            dot(k_ref[end], query[half:], 1, 1),
            dot(v_ref[rows], upstream, 1, 1),
            dot(v_ref[end], upstream[half:], 1, 1),
        )

    def normalize(unit, scores, scores_end, product, product_end):
        first = unit[1] * height
        corner = jnp.where(visible, scores[first:, :half], -jnp.inf)
        corner = jnp.concatenate([corner, scores[first:, half:]], 1)
        scores = corner if first == 0 else jnp.concatenate([scores[:first], corner], 0)
        scores_end = jnp.where(visible, scores_end, -jnp.inf)
        biggest = merge(jnp.max, jnp.maximum, scores, scores_end)
        weights = jnp.exp2((scores - biggest) * power)
        weights_end = jnp.exp2((scores_end - biggest[:, half:]) * power)
        scale = 1.0 / merge(jnp.sum, jnp.add, weights, weights_end)
        center = merge(jnp.sum, jnp.add, weights * product, weights_end * product_end) * scale
        weights = weights * scale
        weights_end = weights_end * scale[:, half:]
        grad = (weights * (product - center) * factor).astype(BF16)
        grad_end = (weights_end * (product_end - center[:, half:]) * factor).astype(BF16)
        return weights.astype(BF16), weights_end.astype(BF16), grad, grad_end

    def collect(unit, weights, weights_end, grad, grad_end):
        query, upstream, rows, end = load(unit)
        columns = slice(unit[0] * depth, (unit[0] + 1) * depth)
        dv_ref[rows] += dot(weights, upstream, 1, 0)
        dv_ref[end] += dot(weights_end, upstream[half:], 1, 0)
        dk_ref[rows] += dot(grad, query, 1, 0)
        dk_ref[end] += dot(grad_end, query[half:], 1, 0)
        query_grad = dot(grad, k_ref[rows], 0, 0)
        tail = query_grad[half:] + dot(grad_end, k_ref[end], 0, 0)
        dq_ref[rows.stop - half : rows.stop, columns] = query_grad[:half].astype(BF16)
        dq_ref[end, columns] = tail.astype(BF16)

    units = [(h, b) for h in range(heads) for b in reversed(range(length // height))]
    held, last = multiply(units[0]), None
    for index, unit in enumerate(units):
        ahead = multiply(units[index + 1]) if index + 1 < len(units) else None
        ready = normalize(unit, *held)
        if last is not None:
            collect(*last)
        last, held = (unit, *ready), ahead
    collect(*last)

    @pl.when(step == pl.num_programs(0) - 1)
    def _():
        mine_ref[...] = jnp.where(is_even, dk_ref[...], dv_ref[...])
        theirs_ref[...] = jnp.where(is_even, dv_ref[...], dk_ref[...])


def attention(own, other, queries, out_grad):
    length, width = queries.shape
    depth = own.shape[1]
    height = min(512, length)
    heads = 2 if width // depth % 2 == 0 else 1
    column = pl.BlockSpec((length, heads * depth), lambda h: (0, h))
    whole = pl.BlockSpec((length, depth), lambda h: (0, 0))
    sums = jax.ShapeDtypeStruct((length, depth), F32)
    return pl.pallas_call(
        functools.partial(attention_kernel, height, heads),
        grid=(width // (heads * depth),),
        in_specs=[whole, whole, column, column],
        out_specs=[column, whole, whole],
        out_shape=[jax.ShapeDtypeStruct((length, width), BF16), sums, sums],
        scratch_shapes=[
            pltpu.VMEM((length, depth), BF16),
            pltpu.VMEM((length, depth), BF16),
            pltpu.VMEM((length, depth), F32),
            pltpu.VMEM((length, depth), F32),
        ],
        compiler_params=IN_ORDER,
        cost_estimate=cost(
            20 * length * length * width,
            6 * queries.nbytes,
            length * length * width // depth,
        ),
        name="attention",
    )(own, other, queries, out_grad)


def spread_kernel(plan, source_ref, *out_refs):
    wide = out_refs[0].shape[1]
    place = lax.axis_index("dp")
    for out, first, step, low, high in plan:
        start = pl.multiple_of((place ^ step) * wide, wide)
        out_refs[out][first : first + high - low] = source_ref[low:high, pl.ds(start, wide)]


def spread(source, wide, plan):
    heights = {}
    for out, first, _, low, high in plan:
        heights[out] = max(heights.get(out, 0), first + high - low)
    return pl.pallas_call(
        functools.partial(spread_kernel, plan),
        out_shape=[
            jax.ShapeDtypeStruct((heights[out], wide), source.dtype) for out in sorted(heights)
        ],
        compiler_params=SMALL,
        cost_estimate=TINY,
        name="spread",
    )(source)


def lay(sources, outputs, hint=TINY):
    def kernel(*refs):
        for out_ref, (_, entries) in zip(refs[len(sources) :], outputs):
            for source, rows, columns, first in entries:
                height = rows.stop - rows.start
                out_ref[first : first + height] = refs[source][rows, columns]

    return pl.pallas_call(
        kernel,
        out_shape=[jax.ShapeDtypeStruct(shape, sources[0].dtype) for shape, _ in outputs],
        compiler_params=SMALL,
        cost_estimate=hint,
        name="lay",
    )(*sources)


def exchange_rows(inputs, wide):
    rows = inputs.shape[0]
    groups = lax.axis_size("dp")
    parts = spread(inputs, wide, [(s, 0, s, 0, rows) for s in range(groups)])
    return [part if s in (0, groups - 1) else swap(part, "dp", s) for s, part in enumerate(parts)]


def product_kernel(jobs, depth, own_ref, other_ref, own_grads_ref, other_grads_ref, *out_refs):
    pairs = ((own_ref, own_grads_ref), (other_ref, other_grads_ref))
    for (places, low, high, _), out_ref in zip(jobs, out_refs):
        columns = slice(places[0] * depth, (places[-1] + 1) * depth)
        total = sum(dot(ref[:, low:high], grads[:, columns], 0, 0) for ref, grads in pairs)
        out_ref[...] = total.astype(out_ref.dtype)


def products(pair, grads, depth, jobs, hint=TINY):
    return pl.pallas_call(
        functools.partial(product_kernel, jobs, depth),
        out_shape=[
            jax.ShapeDtypeStruct((high - low, len(places) * depth), dtype)
            for places, low, high, dtype in jobs
        ],
        compiler_params=SMALL,
        cost_estimate=hint,
        name="products",
    )(*pair, *grads)


def kv_kernel(rows, mine_ref, arrived_ref, mask_ref, *out_refs):
    place = lax.axis_index("tensor")
    chip, core = place // 2, place % 2
    for step, out_ref in enumerate(out_refs):
        for half in range(2):
            start = ((chip ^ step) * 2 + (core ^ half)) * rows
            span = pl.ds(pl.multiple_of(start, rows), rows)
            total = mine_ref[span, :] + arrived_ref[span, :].astype(F32)
            keep = mask_ref[span, :].astype(F32)
            out_ref[half * rows : (half + 1) * rows, :] = (total * keep).astype(BF16)


def kv_blocks(mine, arrived, mask, rows):
    length, depth = mine.shape
    count = length // (2 * rows)
    return pl.pallas_call(
        functools.partial(kv_kernel, rows),
        out_shape=[jax.ShapeDtypeStruct((2 * rows, depth), BF16)] * count,
        compiler_params=SMALL,
        cost_estimate=TINY,
        name="kv_blocks",
    )(mine, arrived, mask)


def per_device(inputs, queries, keys_values, out_grad, weight_mask, clip_mask):
    depth = keys_values.shape[1]
    rows = inputs.shape[0]
    groups = lax.axis_size("dp")
    chips = lax.axis_size("tensor") // 2
    block = weight_mask.shape[0]

    other = swap(keys_values, "tensor", 1)
    parts = exchange_rows(inputs, block)

    query_grad, mine, theirs = attention(keys_values, other, queries, out_grad)
    mine, parts = lax.optimization_barrier((mine, parts))
    arrived = swap(theirs, "tensor", 1)
    blocks = kv_blocks(mine, arrived, clip_mask, rows)

    blocks = [b if s == 0 else swap(b, "tensor", 2 * s) for s, b in enumerate(blocks)]
    parts[-1] = swap(parts[-1], "dp", groups - 1)
    blocks, parts = lax.optimization_barrier((blocks, parts))
    order = sorted(range(chips), key=lambda s: [(s >> b) & 1 for b in range(8)])
    evens, odds = order[: chips // 2], order[chips // 2 :]
    stacked = jnp.concatenate([blocks[s] for s in order], 1)
    found = [stacked if s == 0 else swap(stacked, "dp", s) for s in range(groups)]
    whole = (groups * rows, chips * depth)
    halves = [
        (whole, [(s, slice(h * rows, (h + 1) * rows), slice(None), s * rows) for s in range(groups)])
        for h in (0, 1)
    ]
    grads = lay(found, halves, LONG)

    entries = [(p, slice(0, rows), slice(None), p * rows) for p in range(groups)]
    (packed,) = lay(parts, [((groups * rows, block), entries)])
    pair = (packed, swap(packed, "tensor", 1))

    def send(value, step):
        return swap(value.astype(BF16), "tensor", 2 * step)

    wide, half = block // 2, chips // 2
    far, near = (wide, block), (0, wide)
    away = list(range(2, chips))
    direct = products(pair, grads, depth, [((order.index(s),), *far, BF16) for s in away])
    direct, grads = lax.optimization_barrier((direct, grads))
    (first,) = products(pair, grads, depth, [(range(half, chips), *near, BF16)], LONG)
    direct = [send(value, s) for value, s in zip(direct, away)]
    sent = send(first, 1)
    grads, _ = lax.optimization_barrier((grads, first))
    jobs = [(range(half), *near, F32), ((0,), *far, F32), ((order.index(1),), *far, BF16)]
    even, own, nearest = products(pair, grads, depth, jobs)
    sent, direct = lax.optimization_barrier((sent, direct))
    terms = [even, sent]
    columns, bit = half * depth, 1
    while columns > depth:
        columns, bit = columns // 2, bit * 2
        value = sum(t[:, columns : 2 * columns].astype(F32) for t in terms).astype(BF16)
        terms.append(send(value, bit))
    nearest, _ = lax.optimization_barrier((nearest, value))
    direct.append(send(nearest, 1))
    upper = sum(t[:, :depth].astype(F32) for t in terms)
    lower = own + sum(t.astype(F32) for t in direct)
    summed = jnp.concatenate([upper, lower], 0)
    weight_grad = jnp.where(weight_mask == 1, summed, 0.0)
    return (query_grad, weight_grad)


def solution(mesh):
    spec = P("dp", "tensor")
    in_specs = (P(("dp", "tensor"), None), spec, spec, spec, spec, spec)
    return jax.shard_map(
        per_device, mesh=mesh, in_specs=in_specs, out_specs=(spec, spec), check_vma=False
    )
```

```python
import functools
import math

import jax
import jax.numpy as jnp
from jax import lax
from jax.experimental import pallas as pl
from jax.experimental.pallas import tpu as pltpu
from jax.sharding import PartitionSpec as P

F32 = jnp.float32
BF16 = jnp.bfloat16
VMEM_LIMIT = 40 * 2**20
IN_ORDER = pltpu.CompilerParams(
    vmem_limit_bytes=VMEM_LIMIT, dimension_semantics=("arbitrary",)
)


SMALL = pltpu.CompilerParams(vmem_limit_bytes=16 * 2**20)


def cost(flops, moved, exponents=0):
    return pl.CostEstimate(flops=flops, bytes_accessed=moved, transcendentals=exponents)


TINY, LONG = cost(0, 2**10), cost(2 * 10**10, 2**20)


def swap(value, axis, mask):
    pairs = [(source, source ^ mask) for source in range(lax.axis_size(axis))]
    return lax.ppermute(value, axis, pairs)


def dot(left, right, left_dim, right_dim):
    dims = (((left_dim,), (right_dim,)), ((), ()))
    return lax.dot_general(left, right, dims, preferred_element_type=F32)


def attention_kernel(
    height, heads, own_ref, other_ref, q_ref, up_ref, dq_ref, mine_ref, theirs_ref,
    k_ref, v_ref, dk_ref, dv_ref,
):
    length, depth = k_ref.shape
    factor = depth**-0.5
    power = factor * math.log2(math.e)
    step = pl.program_id(0)
    is_even = lax.axis_index("tensor") % 2 == 0

    @pl.when(step == 0)
    def _():
        k_ref[...] = jnp.where(is_even, own_ref[...], other_ref[...])
        v_ref[...] = jnp.where(is_even, other_ref[...], own_ref[...])
        dk_ref[...] = jnp.zeros_like(dk_ref)
        dv_ref[...] = jnp.zeros_like(dv_ref)

    half = height // 2
    key_place = lax.broadcasted_iota(jnp.int32, (half, half), 0)
    query_place = lax.broadcasted_iota(jnp.int32, (half, half), 1)
    visible = key_place <= query_place

    def merge(reduce, join, long, short):
        long = reduce(long, axis=0, keepdims=True)
        short = reduce(short, axis=0, keepdims=True)
        return jnp.concatenate([long[:, :half], join(long[:, half:], short)], 1)

    def load(unit):
        head, block = unit
        span = slice(block * height, (block + 1) * height)
        columns = slice(head * depth, (head + 1) * depth)
        middle = block * height + half
        rows, end = slice(0, middle), slice(middle, middle + half)
        return q_ref[span, columns], up_ref[span, columns], rows, end

    def multiply(unit):
        query, upstream, rows, end = load(unit)
        return (
            dot(k_ref[rows], query, 1, 1),
            dot(k_ref[end], query[half:], 1, 1),
            dot(v_ref[rows], upstream, 1, 1),
            dot(v_ref[end], upstream[half:], 1, 1),
        )

    def normalize(unit, scores, scores_end, product, product_end):
        first = unit[1] * height
        corner = jnp.where(visible, scores[first:, :half], -jnp.inf)
        corner = jnp.concatenate([corner, scores[first:, half:]], 1)
        scores = corner if first == 0 else jnp.concatenate([scores[:first], corner], 0)
        scores_end = jnp.where(visible, scores_end, -jnp.inf)
        biggest = merge(jnp.max, jnp.maximum, scores, scores_end)
        weights = jnp.exp2((scores - biggest) * power)
        weights_end = jnp.exp2((scores_end - biggest[:, half:]) * power)
        scale = 1.0 / merge(jnp.sum, jnp.add, weights, weights_end)
        center = merge(jnp.sum, jnp.add, weights * product, weights_end * product_end) * scale
        weights = weights * scale
        weights_end = weights_end * scale[:, half:]
        grad = (weights * (product - center) * factor).astype(BF16)
        grad_end = (weights_end * (product_end - center[:, half:]) * factor).astype(BF16)
        return weights.astype(BF16), weights_end.astype(BF16), grad, grad_end

    def collect(unit, weights, weights_end, grad, grad_end):
        query, upstream, rows, end = load(unit)
        columns = slice(unit[0] * depth, (unit[0] + 1) * depth)
        dv_ref[rows] += dot(weights, upstream, 1, 0)
        dv_ref[end] += dot(weights_end, upstream[half:], 1, 0)
        dk_ref[rows] += dot(grad, query, 1, 0)
        dk_ref[end] += dot(grad_end, query[half:], 1, 0)
        query_grad = dot(grad, k_ref[rows], 0, 0)
        tail = query_grad[half:] + dot(grad_end, k_ref[end], 0, 0)
        dq_ref[rows.stop - half : rows.stop, columns] = query_grad[:half].astype(BF16)
        dq_ref[end, columns] = tail.astype(BF16)

    units = [(h, b) for h in range(heads) for b in reversed(range(length // height))]
    held, last = multiply(units[0]), None
    for index, unit in enumerate(units):
        ahead = multiply(units[index + 1]) if index + 1 < len(units) else None
        ready = normalize(unit, *held)
        if last is not None:
            collect(*last)
        last, held = (unit, *ready), ahead
    collect(*last)

    @pl.when(step == pl.num_programs(0) - 1)
    def _():
        mine_ref[...] = jnp.where(is_even, dk_ref[...], dv_ref[...])
        theirs_ref[...] = jnp.where(is_even, dv_ref[...], dk_ref[...])


def attention(own, other, queries, out_grad):
    length, width = queries.shape
    depth = own.shape[1]
    height = min(512, length)
    heads = 2 if width // depth % 2 == 0 else 1
    column = pl.BlockSpec((length, heads * depth), lambda h: (0, h))
    whole = pl.BlockSpec((length, depth), lambda h: (0, 0))
    sums = jax.ShapeDtypeStruct((length, depth), F32)
    return pl.pallas_call(
        functools.partial(attention_kernel, height, heads),
        grid=(width // (heads * depth),),
        in_specs=[whole, whole, column, column],
        out_specs=[column, whole, whole],
        out_shape=[jax.ShapeDtypeStruct((length, width), BF16), sums, sums],
        scratch_shapes=[
            pltpu.VMEM((length, depth), BF16),
            pltpu.VMEM((length, depth), BF16),
            pltpu.VMEM((length, depth), F32),
            pltpu.VMEM((length, depth), F32),
        ],
        compiler_params=IN_ORDER,
        cost_estimate=cost(
            20 * length * length * width,
            6 * queries.nbytes,
            length * length * width // depth,
        ),
        name="attention",
    )(own, other, queries, out_grad)


def spread_kernel(plan, source_ref, *out_refs):
    wide = out_refs[0].shape[1]
    place = lax.axis_index("dp")
    for out, first, step, low, high in plan:
        start = pl.multiple_of((place ^ step) * wide, wide)
        out_refs[out][first : first + high - low] = source_ref[low:high, pl.ds(start, wide)]


def spread(source, wide, plan):
    heights = {}
    for out, first, _, low, high in plan:
        heights[out] = max(heights.get(out, 0), first + high - low)
    return pl.pallas_call(
        functools.partial(spread_kernel, plan),
        out_shape=[
            jax.ShapeDtypeStruct((heights[out], wide), source.dtype) for out in sorted(heights)
        ],
        compiler_params=SMALL,
        cost_estimate=TINY,
        name="spread",
    )(source)


def lay(sources, outputs, hint=TINY):
    def kernel(*refs):
        for out_ref, (_, entries) in zip(refs[len(sources) :], outputs):
            for source, rows, columns, first in entries:
                height = rows.stop - rows.start
                out_ref[first : first + height] = refs[source][rows, columns]

    return pl.pallas_call(
        kernel,
        out_shape=[jax.ShapeDtypeStruct(shape, sources[0].dtype) for shape, _ in outputs],
        compiler_params=SMALL,
        cost_estimate=hint,
        name="lay",
    )(*sources)


def send_rows(inputs, wide):
    rows = inputs.shape[0]
    groups = lax.axis_size("dp")
    if groups != 4:
        parts = spread(inputs, wide, [(s, 0, s, 0, rows) for s in range(groups)])
        return [part if s == 0 else swap(part, "dp", s) for s, part in enumerate(parts)]
    half = rows // 2
    own, left, right = spread(
        inputs,
        wide,
        [(0, 0, 0, 0, rows), (1, 0, 1, 0, rows), (1, rows, 3, 0, half), (2, 0, 2, 0, rows),
         (2, rows, 3, half, rows)],
    )
    return [own, swap(left, "dp", 1), swap(right, "dp", 2)]


def pass_rows(parts, wide):
    rows = parts[0].shape[0]
    groups = lax.axis_size("dp")
    if groups != 4:
        return parts, [[(s, slice(0, rows))] for s in range(groups)]
    own, left, right = parts
    half = rows // 2
    tail = slice(rows, rows + half)
    every = slice(None)
    upper, lower = lay(
        [left, right],
        [((half, wide), [(0, tail, every, 0)]), ((half, wide), [(1, tail, every, 0)])],
    )
    upper, lower = swap(upper, "dp", 2), swap(lower, "dp", 1)
    whole, part = slice(0, rows), slice(0, half)
    places = [[(0, whole)], [(1, whole)], [(2, whole)], [(3, part), (4, part)]]
    return [own, left, right, upper, lower], places


def product_kernel(jobs, depth, held, own_ref, other_ref, *refs):
    grads, out_refs = refs[: 2 * len(held)], refs[2 * len(held) :]

    def pick(steps, half):
        parts = []
        for step in steps:
            group = [step in group for group in held].index(True)
            place = held[group].index(step) * depth
            parts.append(grads[2 * group + half][:, place : place + depth])
        return jnp.concatenate(parts, 1)

    for (steps, low, high, _), out_ref in zip(jobs, out_refs):
        terms = [
            dot(ref[:, low:high], pick(steps, half), 0, 0)
            for half, ref in enumerate((own_ref, other_ref))
        ]
        out_ref[...] = (terms[0] + terms[1]).astype(out_ref.dtype)


def products(pair, found, depth, jobs, hint=TINY):
    return pl.pallas_call(
        functools.partial(product_kernel, jobs, depth, [steps for steps, _ in found]),
        out_shape=[
            jax.ShapeDtypeStruct((high - low, len(steps) * depth), dtype)
            for steps, low, high, dtype in jobs
        ],
        compiler_params=SMALL,
        cost_estimate=hint,
        name="products",
    )(*pair, *[array for _, arrays in found for array in arrays])


def kv_kernel(rows, mine_ref, arrived_ref, mask_ref, *out_refs):
    place = lax.axis_index("tensor")
    chip, core = place // 2, place % 2
    for step, out_ref in enumerate(out_refs):
        for half in range(2):
            start = ((chip ^ step) * 2 + (core ^ half)) * rows
            span = pl.ds(pl.multiple_of(start, rows), rows)
            total = mine_ref[span, :] + arrived_ref[span, :].astype(F32)
            keep = mask_ref[span, :].astype(F32)
            out_ref[half * rows : (half + 1) * rows, :] = (total * keep).astype(BF16)


def kv_blocks(mine, arrived, mask, rows):
    length, depth = mine.shape
    count = length // (2 * rows)
    return pl.pallas_call(
        functools.partial(kv_kernel, rows),
        out_shape=[jax.ShapeDtypeStruct((2 * rows, depth), BF16)] * count,
        compiler_params=SMALL,
        cost_estimate=TINY,
        name="kv_blocks",
    )(mine, arrived, mask)


def per_device(inputs, queries, keys_values, out_grad, weight_mask, clip_mask):
    depth = keys_values.shape[1]
    rows = inputs.shape[0]
    groups = lax.axis_size("dp")
    chips = lax.axis_size("tensor") // 2
    block = weight_mask.shape[0]

    other = swap(keys_values, "tensor", 1)
    parts = send_rows(inputs, block)

    query_grad, mine, theirs = attention(keys_values, other, queries, out_grad)
    mine, parts = lax.optimization_barrier((mine, parts))
    arrived = swap(theirs, "tensor", 1)
    blocks = kv_blocks(mine, arrived, clip_mask, rows)

    blocks = [b if s == 0 else swap(b, "tensor", 2 * s) for s, b in enumerate(blocks)]
    parts, places = pass_rows(parts, block)
    blocks, parts = lax.optimization_barrier((blocks, parts))

    def gather(steps, hint):
        value = jnp.concatenate([blocks[s] for s in steps], 1)
        found = [value if s == 0 else swap(value, "dp", s) for s in range(groups)]
        shape = (groups * rows, value.shape[1])
        outputs = []
        for half in range(2):
            span = slice(half * rows, (half + 1) * rows)
            outputs.append((shape, [(s, span, slice(None), s * rows) for s in range(groups)]))
        return steps, lay(found, outputs, hint)

    found = [gather(tuple(range(chips)), LONG)]

    entries, first = [], 0
    for source in places:
        for array, span in source:
            entries.append((array, span, slice(None), first))
            first += span.stop - span.start
    (packed,) = lay(parts, [((first, block), entries)])
    pair = (packed, swap(packed, "tensor", 1))

    def send(value, step):
        return swap(value.astype(BF16), "tensor", 2 * step)

    wide, half = block // 2, chips // 2
    near, far = (0, wide), (wide, block)
    order = sorted(range(chips), key=lambda s: [(s >> b) & 1 for b in range(8)])

    def after(value):
        arrays, _ = lax.optimization_barrier(([arrays for _, arrays in found], value))
        return [(steps, array) for (steps, _), array in zip(found, arrays)]

    (second,) = products(pair, found, depth, [(tuple(range(half, chips)), *far, BF16)])
    (first,) = products(pair, after(second), depth, [(tuple(order[half:]), *near, BF16)], LONG)
    jobs = [(tuple(order[:half]), *near, F32), (tuple(range(half)), *far, F32)]
    even, low = products(pair, after(first), depth, jobs)

    def reduce(kept, sent, bits):
        terms, columns = [kept, send(sent, bits[0])], half * depth
        for bit in bits[1:]:
            columns //= 2
            value = sum(t[:, columns : 2 * columns].astype(F32) for t in terms).astype(BF16)
            terms.append(send(value, bit))
        return sum(t[:, :depth].astype(F32) for t in terms)

    bits = [2**b for b in range(chips.bit_length() - 1)]
    lower = reduce(low, second, bits[::-1])
    upper = reduce(even, first, bits)
    summed = jnp.concatenate([upper, lower], 0)
    weight_grad = jnp.where(weight_mask == 1, summed, 0.0)
    return (query_grad, weight_grad)


def solution(mesh):
    spec = P("dp", "tensor")
    in_specs = (P(("dp", "tensor"), None), spec, spec, spec, spec, spec)
    return jax.shard_map(
        per_device, mesh=mesh, in_specs=in_specs, out_specs=(spec, spec), check_vma=False
    )
```

```python
import functools
import math

import jax
import jax.numpy as jnp
from jax import lax
from jax.experimental import pallas as pl
from jax.experimental.pallas import tpu as pltpu
from jax.sharding import PartitionSpec as P

F32 = jnp.float32
BF16 = jnp.bfloat16
VMEM_LIMIT = 40 * 2**20
IN_ORDER = pltpu.CompilerParams(
    vmem_limit_bytes=VMEM_LIMIT, dimension_semantics=("arbitrary",)
)


SMALL = pltpu.CompilerParams(vmem_limit_bytes=16 * 2**20)


def cost(flops, moved, exponents=0):
    return pl.CostEstimate(flops=flops, bytes_accessed=moved, transcendentals=exponents)


TINY, LONG = cost(0, 2**10), cost(2 * 10**10, 2**20)


def swap(value, axis, mask):
    pairs = [(source, source ^ mask) for source in range(lax.axis_size(axis))]
    return lax.ppermute(value, axis, pairs)


def dot(left, right, left_dim, right_dim):
    dims = (((left_dim,), (right_dim,)), ((), ()))
    return lax.dot_general(left, right, dims, preferred_element_type=F32)


def attention_kernel(
    height, heads, own_ref, other_ref, q_ref, up_ref, dq_ref, mine_ref, theirs_ref,
    k_ref, v_ref, dk_ref, dv_ref,
):
    length, depth = k_ref.shape
    factor = depth**-0.5
    power = factor * math.log2(math.e)
    step = pl.program_id(0)
    is_even = lax.axis_index("tensor") % 2 == 0

    @pl.when(step == 0)
    def _():
        k_ref[...] = jnp.where(is_even, own_ref[...], other_ref[...])
        v_ref[...] = jnp.where(is_even, other_ref[...], own_ref[...])
        dk_ref[...] = jnp.zeros_like(dk_ref)
        dv_ref[...] = jnp.zeros_like(dv_ref)

    half = height // 2
    key_place = lax.broadcasted_iota(jnp.int32, (half, half), 0)
    query_place = lax.broadcasted_iota(jnp.int32, (half, half), 1)
    visible = key_place <= query_place

    def merge(reduce, join, long, short):
        long = reduce(long, axis=0, keepdims=True)
        short = reduce(short, axis=0, keepdims=True)
        return jnp.concatenate([long[:, :half], join(long[:, half:], short)], 1)

    def load(unit):
        head, block = unit
        span = slice(block * height, (block + 1) * height)
        columns = slice(head * depth, (head + 1) * depth)
        middle = block * height + half
        rows, end = slice(0, middle), slice(middle, middle + half)
        return q_ref[span, columns], up_ref[span, columns], rows, end

    def multiply(unit):
        query, upstream, rows, end = load(unit)
        return (
            dot(k_ref[rows], query, 1, 1),
            dot(k_ref[end], query[half:], 1, 1),
            dot(v_ref[rows], upstream, 1, 1),
            dot(v_ref[end], upstream[half:], 1, 1),
        )

    def normalize(unit, scores, scores_end, product, product_end):
        first = unit[1] * height
        corner = jnp.where(visible, scores[first:, :half], -jnp.inf)
        corner = jnp.concatenate([corner, scores[first:, half:]], 1)
        scores = corner if first == 0 else jnp.concatenate([scores[:first], corner], 0)
        scores_end = jnp.where(visible, scores_end, -jnp.inf)
        biggest = merge(jnp.max, jnp.maximum, scores, scores_end)
        weights = jnp.exp2((scores - biggest) * power)
        weights_end = jnp.exp2((scores_end - biggest[:, half:]) * power)
        scale = 1.0 / merge(jnp.sum, jnp.add, weights, weights_end)
        center = merge(jnp.sum, jnp.add, weights * product, weights_end * product_end) * scale
        weights = weights * scale
        weights_end = weights_end * scale[:, half:]
        grad = (weights * (product - center) * factor).astype(BF16)
        grad_end = (weights_end * (product_end - center[:, half:]) * factor).astype(BF16)
        return weights.astype(BF16), weights_end.astype(BF16), grad, grad_end

    def collect(unit, weights, weights_end, grad, grad_end):
        query, upstream, rows, end = load(unit)
        columns = slice(unit[0] * depth, (unit[0] + 1) * depth)
        dv_ref[rows] += dot(weights, upstream, 1, 0)
        dv_ref[end] += dot(weights_end, upstream[half:], 1, 0)
        dk_ref[rows] += dot(grad, query, 1, 0)
        dk_ref[end] += dot(grad_end, query[half:], 1, 0)
        query_grad = dot(grad, k_ref[rows], 0, 0)
        tail = query_grad[half:] + dot(grad_end, k_ref[end], 0, 0)
        dq_ref[rows.stop - half : rows.stop, columns] = query_grad[:half].astype(BF16)
        dq_ref[end, columns] = tail.astype(BF16)

    units = [(h, b) for h in range(heads) for b in reversed(range(length // height))]
    held, last = multiply(units[0]), None
    for index, unit in enumerate(units):
        ahead = multiply(units[index + 1]) if index + 1 < len(units) else None
        ready = normalize(unit, *held)
        if last is not None:
            collect(*last)
        last, held = (unit, *ready), ahead
    collect(*last)

    @pl.when(step == pl.num_programs(0) - 1)
    def _():
        mine_ref[...] = jnp.where(is_even, dk_ref[...], dv_ref[...])
        theirs_ref[...] = jnp.where(is_even, dv_ref[...], dk_ref[...])


def attention(own, other, queries, out_grad):
    length, width = queries.shape
    depth = own.shape[1]
    height = min(512, length)
    heads = 2 if width // depth % 2 == 0 else 1
    column = pl.BlockSpec((length, heads * depth), lambda h: (0, h))
    whole = pl.BlockSpec((length, depth), lambda h: (0, 0))
    sums = jax.ShapeDtypeStruct((length, depth), F32)
    return pl.pallas_call(
        functools.partial(attention_kernel, height, heads),
        grid=(width // (heads * depth),),
        in_specs=[whole, whole, column, column],
        out_specs=[column, whole, whole],
        out_shape=[jax.ShapeDtypeStruct((length, width), BF16), sums, sums],
        scratch_shapes=[
            pltpu.VMEM((length, depth), BF16),
            pltpu.VMEM((length, depth), BF16),
            pltpu.VMEM((length, depth), F32),
            pltpu.VMEM((length, depth), F32),
        ],
        compiler_params=IN_ORDER,
        cost_estimate=cost(
            20 * length * length * width,
            6 * queries.nbytes,
            length * length * width // depth,
        ),
        name="attention",
    )(own, other, queries, out_grad)


def spread_kernel(plan, source_ref, *out_refs):
    wide = out_refs[0].shape[1]
    place = lax.axis_index("dp")
    for out, first, step, low, high in plan:
        start = pl.multiple_of((place ^ step) * wide, wide)
        out_refs[out][first : first + high - low] = source_ref[low:high, pl.ds(start, wide)]


def spread(source, wide, plan):
    heights = {}
    for out, first, _, low, high in plan:
        heights[out] = max(heights.get(out, 0), first + high - low)
    return pl.pallas_call(
        functools.partial(spread_kernel, plan),
        out_shape=[
            jax.ShapeDtypeStruct((heights[out], wide), source.dtype) for out in sorted(heights)
        ],
        compiler_params=SMALL,
        cost_estimate=TINY,
        name="spread",
    )(source)


def lay(sources, outputs, hint=TINY):
    def kernel(*refs):
        for out_ref, (_, entries) in zip(refs[len(sources) :], outputs):
            for source, rows, columns, first in entries:
                height = rows.stop - rows.start
                out_ref[first : first + height] = refs[source][rows, columns]

    return pl.pallas_call(
        kernel,
        out_shape=[jax.ShapeDtypeStruct(shape, sources[0].dtype) for shape, _ in outputs],
        compiler_params=SMALL,
        cost_estimate=hint,
        name="lay",
    )(*sources)


def send_rows(inputs, wide):
    rows = inputs.shape[0]
    groups = lax.axis_size("dp")
    if groups != 4:
        parts = spread(inputs, wide, [(s, 0, s, 0, rows) for s in range(groups)])
        return [part if s == 0 else swap(part, "dp", s) for s, part in enumerate(parts)]
    half = rows // 2
    own, left, right = spread(
        inputs,
        wide,
        [(0, 0, 0, 0, rows), (1, 0, 1, 0, rows), (1, rows, 3, 0, half), (2, 0, 2, 0, rows),
         (2, rows, 3, half, rows)],
    )
    return [own, swap(left, "dp", 1), swap(right, "dp", 2)]


def pass_rows(parts, wide):
    rows = parts[0].shape[0]
    groups = lax.axis_size("dp")
    if groups != 4:
        return parts, [[(s, slice(0, rows))] for s in range(groups)]
    own, left, right = parts
    half = rows // 2
    tail = slice(rows, rows + half)
    every = slice(None)
    upper, lower = lay(
        [left, right],
        [((half, wide), [(0, tail, every, 0)]), ((half, wide), [(1, tail, every, 0)])],
    )
    upper, lower = swap(upper, "dp", 2), swap(lower, "dp", 1)
    whole, part = slice(0, rows), slice(0, half)
    places = [[(0, whole)], [(1, whole)], [(2, whole)], [(3, part), (4, part)]]
    return [own, left, right, upper, lower], places


def product_kernel(jobs, depth, held, own_ref, other_ref, *refs):
    grads, out_refs = refs[: 2 * len(held)], refs[2 * len(held) :]

    def pick(steps, half):
        parts = []
        for step in steps:
            group = [step in group for group in held].index(True)
            place = held[group].index(step) * depth
            parts.append(grads[2 * group + half][:, place : place + depth])
        return jnp.concatenate(parts, 1)

    for (steps, low, high, _), out_ref in zip(jobs, out_refs):
        terms = [
            dot(ref[:, low:high], pick(steps, half), 0, 0)
            for half, ref in enumerate((own_ref, other_ref))
        ]
        out_ref[...] = (terms[0] + terms[1]).astype(out_ref.dtype)


def products(pair, found, depth, jobs, hint=TINY):
    return pl.pallas_call(
        functools.partial(product_kernel, jobs, depth, [steps for steps, _ in found]),
        out_shape=[
            jax.ShapeDtypeStruct((high - low, len(steps) * depth), dtype)
            for steps, low, high, dtype in jobs
        ],
        compiler_params=SMALL,
        cost_estimate=hint,
        name="products",
    )(*pair, *[array for _, arrays in found for array in arrays])


def kv_kernel(rows, mine_ref, arrived_ref, mask_ref, *out_refs):
    place = lax.axis_index("tensor")
    chip, core = place // 2, place % 2
    for step, out_ref in enumerate(out_refs):
        for half in range(2):
            start = ((chip ^ step) * 2 + (core ^ half)) * rows
            span = pl.ds(pl.multiple_of(start, rows), rows)
            total = mine_ref[span, :] + arrived_ref[span, :].astype(F32)
            keep = mask_ref[span, :].astype(F32)
            out_ref[half * rows : (half + 1) * rows, :] = (total * keep).astype(BF16)


def kv_blocks(mine, arrived, mask, rows):
    length, depth = mine.shape
    count = length // (2 * rows)
    return pl.pallas_call(
        functools.partial(kv_kernel, rows),
        out_shape=[jax.ShapeDtypeStruct((2 * rows, depth), BF16)] * count,
        compiler_params=SMALL,
        cost_estimate=TINY,
        name="kv_blocks",
    )(mine, arrived, mask)


def per_device(inputs, queries, keys_values, out_grad, weight_mask, clip_mask):
    depth = keys_values.shape[1]
    rows = inputs.shape[0]
    groups = lax.axis_size("dp")
    chips = lax.axis_size("tensor") // 2
    block = weight_mask.shape[0]

    other = swap(keys_values, "tensor", 1)
    parts = send_rows(inputs, block)

    query_grad, mine, theirs = attention(keys_values, other, queries, out_grad)
    mine, parts = lax.optimization_barrier((mine, parts))
    arrived = swap(theirs, "tensor", 1)
    blocks = kv_blocks(mine, arrived, clip_mask, rows)

    blocks = [b if s == 0 else swap(b, "tensor", 2 * s) for s, b in enumerate(blocks)]
    parts, places = pass_rows(parts, block)
    blocks, parts = lax.optimization_barrier((blocks, parts))

    def gather(steps, hint):
        value = jnp.concatenate([blocks[s] for s in steps], 1)
        shape = (groups * rows, value.shape[1])
        every = slice(None)
        spans = [slice(half * rows, (half + 1) * rows) for half in range(2)]
        if groups != 4:
            found = [value if s == 0 else swap(value, "dp", s) for s in range(groups)]
            outputs = [
                (shape, [(s, span, every, s * rows) for s in range(groups)]) for span in spans
            ]
            return steps, lay(found, outputs, hint)
        left, right = swap(value, "dp", 1), swap(value, "dp", 2)
        piece = (rows, value.shape[1])
        passed = [(piece, [(1, spans[0], every, 0)]), (piece, [(0, spans[1], every, 0)])]
        upper, lower = lay([left, right], passed)
        found = [value, left, right, swap(upper, "dp", 1), swap(lower, "dp", 2)]
        outputs = []
        for half, span in enumerate(spans):
            entries = [(s, span, every, s * rows) for s in range(3)]
            outputs.append((shape, entries + [(3 + half, spans[0], every, 3 * rows)]))
        return steps, lay(found, outputs, hint)

    found = [gather(tuple(range(chips)), LONG)]

    entries, first = [], 0
    for source in places:
        for array, span in source:
            entries.append((array, span, slice(None), first))
            first += span.stop - span.start
    (packed,) = lay(parts, [((first, block), entries)])
    pair = (packed, swap(packed, "tensor", 1))

    def send(value, step):
        return swap(value.astype(BF16), "tensor", 2 * step)

    wide, half = block // 2, chips // 2
    near, far = (0, wide), (wide, block)
    order = sorted(range(chips), key=lambda s: [(s >> b) & 1 for b in range(8)])

    def after(value):
        arrays, _ = lax.optimization_barrier(([arrays for _, arrays in found], value))
        return [(steps, array) for (steps, _), array in zip(found, arrays)]

    (second,) = products(pair, found, depth, [(tuple(range(half, chips)), *far, BF16)])
    (first,) = products(pair, after(second), depth, [(tuple(order[half:]), *near, BF16)], LONG)
    jobs = [(tuple(order[:half]), *near, F32), (tuple(range(half)), *far, F32)]
    even, low = products(pair, after(first), depth, jobs)

    def reduce(kept, sent, bits):
        terms, columns = [kept, send(sent, bits[0])], half * depth
        for bit in bits[1:]:
            columns //= 2
            value = sum(t[:, columns : 2 * columns].astype(F32) for t in terms).astype(BF16)
            terms.append(send(value, bit))
        return sum(t[:, :depth].astype(F32) for t in terms)

    bits = [2**b for b in range(chips.bit_length() - 1)]
    lower = reduce(low, second, bits[::-1])
    upper = reduce(even, first, bits)
    summed = jnp.concatenate([upper, lower], 0)
    weight_grad = jnp.where(weight_mask == 1, summed, 0.0)
    return (query_grad, weight_grad)


def solution(mesh):
    spec = P("dp", "tensor")
    in_specs = (P(("dp", "tensor"), None), spec, spec, spec, spec, spec)
    return jax.shard_map(
        per_device, mesh=mesh, in_specs=in_specs, out_specs=(spec, spec), check_vma=False
    )
```

```python
import functools
import math

import jax
import jax.numpy as jnp
from jax import lax
from jax.experimental import pallas as pl
from jax.experimental.pallas import tpu as pltpu
from jax.sharding import PartitionSpec as P

F32 = jnp.float32
BF16 = jnp.bfloat16
VMEM_LIMIT = 40 * 2**20
IN_ORDER = pltpu.CompilerParams(
    vmem_limit_bytes=VMEM_LIMIT, dimension_semantics=("arbitrary",)
)


SMALL = pltpu.CompilerParams(vmem_limit_bytes=16 * 2**20)


def cost(flops, moved, exponents=0):
    return pl.CostEstimate(flops=flops, bytes_accessed=moved, transcendentals=exponents)


TINY, LONG = cost(0, 2**10), cost(2 * 10**10, 2**20)


def swap(value, axis, mask):
    pairs = [(source, source ^ mask) for source in range(lax.axis_size(axis))]
    return lax.ppermute(value, axis, pairs)


def dot(left, right, left_dim, right_dim):
    dims = (((left_dim,), (right_dim,)), ((), ()))
    return lax.dot_general(left, right, dims, preferred_element_type=F32)


def attention_kernel(
    height, heads, own_ref, other_ref, q_ref, up_ref, dq_ref, mine_ref, theirs_ref,
    k_ref, v_ref, dk_ref, dv_ref,
):
    length, depth = k_ref.shape
    factor = depth**-0.5
    power = factor * math.log2(math.e)
    step = pl.program_id(0)
    is_even = lax.axis_index("tensor") % 2 == 0

    @pl.when(step == 0)
    def _():
        k_ref[...] = jnp.where(is_even, own_ref[...], other_ref[...])
        v_ref[...] = jnp.where(is_even, other_ref[...], own_ref[...])
        dk_ref[...] = jnp.zeros_like(dk_ref)
        dv_ref[...] = jnp.zeros_like(dv_ref)

    half = height // 2
    key_place = lax.broadcasted_iota(jnp.int32, (half, half), 0)
    query_place = lax.broadcasted_iota(jnp.int32, (half, half), 1)
    visible = key_place <= query_place

    def merge(reduce, join, long, short):
        long = reduce(long, axis=0, keepdims=True)
        short = reduce(short, axis=0, keepdims=True)
        return jnp.concatenate([long[:, :half], join(long[:, half:], short)], 1)

    def load(unit):
        head, block = unit
        span = slice(block * height, (block + 1) * height)
        columns = slice(head * depth, (head + 1) * depth)
        middle = block * height + half
        rows, end = slice(0, middle), slice(middle, middle + half)
        return q_ref[span, columns], up_ref[span, columns], rows, end

    def multiply(unit):
        query, upstream, rows, end = load(unit)
        return (
            dot(k_ref[rows], query, 1, 1),
            dot(k_ref[end], query[half:], 1, 1),
            dot(v_ref[rows], upstream, 1, 1),
            dot(v_ref[end], upstream[half:], 1, 1),
        )

    def normalize(unit, scores, scores_end, product, product_end):
        first = unit[1] * height
        corner = jnp.where(visible, scores[first:, :half], -jnp.inf)
        corner = jnp.concatenate([corner, scores[first:, half:]], 1)
        scores = corner if first == 0 else jnp.concatenate([scores[:first], corner], 0)
        scores_end = jnp.where(visible, scores_end, -jnp.inf)
        biggest = merge(jnp.max, jnp.maximum, scores, scores_end)
        weights = jnp.exp2((scores - biggest) * power)
        weights_end = jnp.exp2((scores_end - biggest[:, half:]) * power)
        scale = 1.0 / merge(jnp.sum, jnp.add, weights, weights_end)
        center = merge(jnp.sum, jnp.add, weights * product, weights_end * product_end) * scale
        weights = weights * scale
        weights_end = weights_end * scale[:, half:]
        grad = (weights * (product - center) * factor).astype(BF16)
        grad_end = (weights_end * (product_end - center[:, half:]) * factor).astype(BF16)
        return weights.astype(BF16), weights_end.astype(BF16), grad, grad_end

    def collect(unit, weights, weights_end, grad, grad_end):
        query, upstream, rows, end = load(unit)
        columns = slice(unit[0] * depth, (unit[0] + 1) * depth)
        dv_ref[rows] += dot(weights, upstream, 1, 0)
        dv_ref[end] += dot(weights_end, upstream[half:], 1, 0)
        dk_ref[rows] += dot(grad, query, 1, 0)
        dk_ref[end] += dot(grad_end, query[half:], 1, 0)
        query_grad = dot(grad, k_ref[rows], 0, 0)
        tail = query_grad[half:] + dot(grad_end, k_ref[end], 0, 0)
        dq_ref[rows.stop - half : rows.stop, columns] = query_grad[:half].astype(BF16)
        dq_ref[end, columns] = tail.astype(BF16)

    units = [(h, b) for h in range(heads) for b in reversed(range(length // height))]
    held, last = multiply(units[0]), None
    for index, unit in enumerate(units):
        ahead = multiply(units[index + 1]) if index + 1 < len(units) else None
        ready = normalize(unit, *held)
        if last is not None:
            collect(*last)
        last, held = (unit, *ready), ahead
    collect(*last)

    @pl.when(step == pl.num_programs(0) - 1)
    def _():
        mine_ref[...] = jnp.where(is_even, dk_ref[...], dv_ref[...])
        theirs_ref[...] = jnp.where(is_even, dv_ref[...], dk_ref[...]).astype(BF16)


def attention(own, other, queries, out_grad):
    length, width = queries.shape
    depth = own.shape[1]
    height = min(512, length)
    heads = 2 if width // depth % 2 == 0 else 1
    column = pl.BlockSpec((length, heads * depth), lambda h: (0, h))
    whole = pl.BlockSpec((length, depth), lambda h: (0, 0))
    sums = jax.ShapeDtypeStruct((length, depth), F32)
    return pl.pallas_call(
        functools.partial(attention_kernel, height, heads),
        grid=(width // (heads * depth),),
        in_specs=[whole, whole, column, column],
        out_specs=[column, whole, whole],
        out_shape=[
            jax.ShapeDtypeStruct((length, width), BF16),
            sums,
            jax.ShapeDtypeStruct((length, depth), BF16),
        ],
        scratch_shapes=[
            pltpu.VMEM((length, depth), BF16),
            pltpu.VMEM((length, depth), BF16),
            pltpu.VMEM((length, depth), F32),
            pltpu.VMEM((length, depth), F32),
        ],
        compiler_params=IN_ORDER,
        cost_estimate=cost(
            20 * length * length * width,
            6 * queries.nbytes,
            length * length * width // depth,
        ),
        name="attention",
    )(own, other, queries, out_grad)


def spread_kernel(plan, source_ref, *out_refs):
    wide = out_refs[0].shape[1]
    place = lax.axis_index("dp")
    for out, first, step, low, high in plan:
        start = pl.multiple_of((place ^ step) * wide, wide)
        out_refs[out][first : first + high - low] = source_ref[low:high, pl.ds(start, wide)]


def spread(source, wide, plan):
    heights = {}
    for out, first, _, low, high in plan:
        heights[out] = max(heights.get(out, 0), first + high - low)
    return pl.pallas_call(
        functools.partial(spread_kernel, plan),
        out_shape=[
            jax.ShapeDtypeStruct((heights[out], wide), source.dtype) for out in sorted(heights)
        ],
        compiler_params=SMALL,
        cost_estimate=TINY,
        name="spread",
    )(source)


def lay(sources, outputs, hint=TINY):
    def kernel(*refs):
        for out_ref, (_, entries) in zip(refs[len(sources) :], outputs):
            for source, rows, columns, first in entries:
                height = rows.stop - rows.start
                out_ref[first : first + height] = refs[source][rows, columns]

    return pl.pallas_call(
        kernel,
        out_shape=[jax.ShapeDtypeStruct(shape, sources[0].dtype) for shape, _ in outputs],
        compiler_params=SMALL,
        cost_estimate=hint,
        name="lay",
    )(*sources)


def send_rows(inputs, wide):
    rows = inputs.shape[0]
    groups = lax.axis_size("dp")
    if groups != 4:
        parts = spread(inputs, wide, [(s, 0, s, 0, rows) for s in range(groups)])
        return [part if s == 0 else swap(part, "dp", s) for s, part in enumerate(parts)]
    half = rows // 2
    own, left, right = spread(
        inputs,
        wide,
        [(0, 0, 0, 0, rows), (1, 0, 1, 0, rows), (1, rows, 3, 0, half), (2, 0, 2, 0, rows),
         (2, rows, 3, half, rows)],
    )
    return [own, swap(left, "dp", 1), swap(right, "dp", 2)]


def pass_rows(parts, wide):
    rows = parts[0].shape[0]
    groups = lax.axis_size("dp")
    if groups != 4:
        return parts, [[(s, slice(0, rows))] for s in range(groups)]
    own, left, right = parts
    half = rows // 2
    tail = slice(rows, rows + half)
    every = slice(None)
    upper, lower = lay(
        [left, right],
        [((half, wide), [(0, tail, every, 0)]), ((half, wide), [(1, tail, every, 0)])],
    )
    upper, lower = swap(upper, "dp", 2), swap(lower, "dp", 1)
    whole, part = slice(0, rows), slice(0, half)
    places = [[(0, whole)], [(1, whole)], [(2, whole)], [(3, part), (4, part)]]
    return [own, left, right, upper, lower], places


def product_kernel(jobs, depth, held, own_ref, other_ref, *refs):
    grads, out_refs = refs[: 2 * len(held)], refs[2 * len(held) :]

    def pick(steps, half):
        parts = []
        for step in steps:
            group = [step in group for group in held].index(True)
            place = held[group].index(step) * depth
            parts.append(grads[2 * group + half][:, place : place + depth])
        return jnp.concatenate(parts, 1)

    for (steps, low, high, _), out_ref in zip(jobs, out_refs):
        terms = [
            dot(ref[:, low:high], pick(steps, half), 0, 0)
            for half, ref in enumerate((own_ref, other_ref))
        ]
        out_ref[...] = (terms[0] + terms[1]).astype(out_ref.dtype)


def products(pair, found, depth, jobs, hint=TINY):
    return pl.pallas_call(
        functools.partial(product_kernel, jobs, depth, [steps for steps, _ in found]),
        out_shape=[
            jax.ShapeDtypeStruct((high - low, len(steps) * depth), dtype)
            for steps, low, high, dtype in jobs
        ],
        compiler_params=SMALL,
        cost_estimate=hint,
        name="products",
    )(*pair, *[array for _, arrays in found for array in arrays])


def kv_kernel(rows, mine_ref, arrived_ref, mask_ref, *out_refs):
    place = lax.axis_index("tensor")
    chip, core = place // 2, place % 2
    for step, out_ref in enumerate(out_refs):
        for half in range(2):
            start = ((chip ^ step) * 2 + (core ^ half)) * rows
            span = pl.ds(pl.multiple_of(start, rows), rows)
            total = mine_ref[span, :] + arrived_ref[span, :].astype(F32).astype(F32)
            keep = mask_ref[span, :].astype(F32)
            out_ref[half * rows : (half + 1) * rows, :] = (total * keep).astype(BF16)


def kv_blocks(mine, arrived, mask, rows):
    length, depth = mine.shape
    count = length // (2 * rows)
    return pl.pallas_call(
        functools.partial(kv_kernel, rows),
        out_shape=[jax.ShapeDtypeStruct((2 * rows, depth), BF16)] * count,
        compiler_params=SMALL,
        cost_estimate=TINY,
        name="kv_blocks",
    )(mine, arrived, mask)


def per_device(inputs, queries, keys_values, out_grad, weight_mask, clip_mask):
    depth = keys_values.shape[1]
    rows = inputs.shape[0]
    groups = lax.axis_size("dp")
    chips = lax.axis_size("tensor") // 2
    block = weight_mask.shape[0]

    other = swap(keys_values, "tensor", 1)
    parts = send_rows(inputs, block)

    query_grad, mine, theirs = attention(keys_values, other, queries, out_grad)
    mine, parts = lax.optimization_barrier((mine, parts))
    arrived = swap(theirs, "tensor", 1)
    blocks = kv_blocks(mine, arrived, clip_mask, rows)

    blocks = [b if s == 0 else swap(b, "tensor", 2 * s) for s, b in enumerate(blocks)]
    parts, places = pass_rows(parts, block)
    blocks, parts = lax.optimization_barrier((blocks, parts))

    def gather(steps, hint):
        value = jnp.concatenate([blocks[s] for s in steps], 1)
        shape = (groups * rows, value.shape[1])
        every = slice(None)
        spans = [slice(half * rows, (half + 1) * rows) for half in range(2)]
        if groups != 4:
            found = [value if s == 0 else swap(value, "dp", s) for s in range(groups)]
            outputs = [
                (shape, [(s, span, every, s * rows) for s in range(groups)]) for span in spans
            ]
            return steps, lay(found, outputs, hint)
        left, right = swap(value, "dp", 1), swap(value, "dp", 2)
        piece = (rows, value.shape[1])
        passed = [(piece, [(1, spans[0], every, 0)]), (piece, [(0, spans[1], every, 0)])]
        upper, lower = lay([left, right], passed)
        found = [value, left, right, swap(upper, "dp", 1), swap(lower, "dp", 2)]
        outputs = []
        for half, span in enumerate(spans):
            entries = [(s, span, every, s * rows) for s in range(3)]
            outputs.append((shape, entries + [(3 + half, spans[0], every, 3 * rows)]))
        return steps, lay(found, outputs, hint)

    found = [gather(tuple(range(chips)), LONG)]

    entries, first = [], 0
    for source in places:
        for array, span in source:
            entries.append((array, span, slice(None), first))
            first += span.stop - span.start
    (packed,) = lay(parts, [((first, block), entries)])
    pair = (packed, swap(packed, "tensor", 1))

    def send(value, step):
        return swap(value.astype(BF16), "tensor", 2 * step)

    wide, half = block // 2, chips // 2
    near, far = (0, wide), (wide, block)
    order = sorted(range(chips), key=lambda s: [(s >> b) & 1 for b in range(8)])

    def after(value):
        arrays, _ = lax.optimization_barrier(([arrays for _, arrays in found], value))
        return [(steps, array) for (steps, _), array in zip(found, arrays)]

    (second,) = products(pair, found, depth, [(tuple(range(half, chips)), *far, BF16)])
    (first,) = products(pair, after(second), depth, [(tuple(order[half:]), *near, BF16)], LONG)
    jobs = [(tuple(order[:half]), *near, F32), (tuple(range(half)), *far, F32)]
    even, low = products(pair, after(first), depth, jobs)

    def reduce(kept, sent, bits):
        terms, columns = [kept, send(sent, bits[0])], half * depth
        for bit in bits[1:]:
            columns //= 2
            value = sum(t[:, columns : 2 * columns].astype(F32) for t in terms).astype(BF16)
            terms.append(send(value, bit))
        return sum(t[:, :depth].astype(F32) for t in terms)

    bits = [2**b for b in range(chips.bit_length() - 1)]
    lower = reduce(low, second, bits[::-1])
    upper = reduce(even, first, bits)
    summed = jnp.concatenate([upper, lower], 0)
    weight_grad = jnp.where(weight_mask == 1, summed, 0.0)
    return (query_grad, weight_grad)


def solution(mesh):
    spec = P("dp", "tensor")
    in_specs = (P(("dp", "tensor"), None), spec, spec, spec, spec, spec)
    return jax.shard_map(
        per_device, mesh=mesh, in_specs=in_specs, out_specs=(spec, spec), check_vma=False
    )
```
